32 devices in a mesh: seq: 4 (over y, x), head: 8 (over z, core).
Axes of the slice: x: 2, y: 2, z: 4, core: 2. Of those that a mesh axis runs over, the one named last changes fastest.
Arguments:
- queries: bfloat16 [8192, 4096], P('seq', 'head'), may hold values from -80 to 80
- transposed_keys: bfloat16 [512, 8192], P('head', 'seq'), may hold values from -25 to 25
- transposed_values: bfloat16 [512, 8192], P('head', 'seq'), may hold values from -6 to 6
- adapter_down_factor: bfloat16 [4096, 64], P('head'), may hold values from -0.5 to 0.5
- adapter_up_factor: bfloat16 [64, 4096], P(None, 'head'), may hold values from -0.75 to 0.75
- projection_output_gradient: bfloat16 [8192, 4096], P('seq', 'head'), may hold values from -0.0625 to 0.0625
Outputs:
- adapter_activations: float32 [64, 8192], P(None, 'seq')
- down_factor_gradient: float32 [4096, 64], P('head')
- up_factor_gradient: float32 [64, 4096], P(None, 'head')
The draws below stay inside these ranges and needn't reach their ends.
All inputs are finite; a program needn't handle non-finite values.
Results may differ from the reference program's by a relative error of at most 0.0046.
Values may be sent and summed in bfloat16 or wider, within the bound.
A program may use at most 64 MiB of HBM per device.

```python
import math
import jax
import jax.numpy as jnp
from jax import lax

GROUP = 2048
HALF = 1024
SEQ_LEN = 8192
HEAD_SIZE = 128
H = 32
KVH = 4
MODEL_WIDTH = 4096
ADAPTER_RANK = 64


def joint_draw(key):
    query_seed = jax.random.fold_in(key, 11)
    keys_seed = jax.random.fold_in(key, 23)
    base_query = jax.random.truncated_normal(query_seed, -6.0, 6.0, (SEQ_LEN, MODEL_WIDTH), jnp.float32)
    base_key = jax.random.truncated_normal(keys_seed, -6.0, 6.0, (KVH * HEAD_SIZE, SEQ_LEN), jnp.float32)
    return (base_query, base_key)


def draw_queries(key, part):
    return joint_draw(key)[0].astype(jnp.bfloat16)


def draw_transposed_keys(key, part):
    return joint_draw(key)[1].astype(jnp.bfloat16)


def level_of(rng, dims, shards, smallest, high):
    level, own = 1.0, jax.random.fold_in(rng, 6)
    for dim, blocks in shards:
        draws = jnp.exp(jax.random.uniform(jax.random.fold_in(own, dim), (blocks,), jnp.float32, smallest / len(shards), high / len(shards)))
        level = level * jnp.repeat(draws, dims[dim] // blocks).reshape([-1 if axis == dim else 1 for axis in range(len(dims))])
    return level


def gaussian(own_key, shape, scale, limit, cuts=(), held_as=jnp.bfloat16):
    gain = level_of(own_key, shape, cuts, -0.22, 0.18) if cuts else 1.0
    entries = jax.random.normal(own_key, shape, jnp.float32) * scale * gain
    return jnp.minimum(jnp.maximum(entries, -limit), limit).astype(held_as)


def setup_inputs(seed: int = 0) -> dict:
    key_of = jax.random.split(jax.random.key(seed), 7)
    return {
        "queries": draw_queries(jax.random.fold_in(key_of[6], 71), 0),
        "transposed_keys": draw_transposed_keys(jax.random.fold_in(key_of[6], 71), 0),
        "transposed_values": gaussian(key_of[2], (KVH * HEAD_SIZE, SEQ_LEN), 1.0, 6.0, ((0, 8), (1, 4))),
        "adapter_down_factor": gaussian(key_of[3], (MODEL_WIDTH, ADAPTER_RANK), HEAD_SIZE ** -0.5, 0.5, ((0, 8),)),
        "adapter_up_factor": gaussian(key_of[4], (ADAPTER_RANK, MODEL_WIDTH), ADAPTER_RANK ** -0.5, 0.75, ((1, 8),)),
        "projection_output_gradient": gaussian(key_of[5], (SEQ_LEN, MODEL_WIDTH), SEQ_LEN ** -0.5, 0.0625, ((0, 4), (1, 8))),
    }


neg_big = -1e+30
adapter_scale = 2.0

def group_attend(operands):
    group_query, group_key, group_value = operands
    scores = jnp.dot(group_query, group_key, preferred_element_type=jnp.float32) * (1.0 / math.sqrt(HEAD_SIZE))
    visible = jnp.arange(GROUP)[:, None] >= jnp.arange(GROUP)[None, :]
    masked = jnp.where(visible, scores, neg_big)
    row_max = lax.optimization_barrier(jnp.max(masked, axis=1, keepdims=True))
    weights = jnp.exp(masked - row_max)
    totals = lax.optimization_barrier(jnp.sum(weights, axis=1, keepdims=True))
    rounded = weights.astype(jnp.bfloat16)
    context = jnp.dot(rounded, group_value.T, preferred_element_type=jnp.float32) / totals
    return context.astype(jnp.bfloat16)

def one_head(head_index, queries, transposed_keys, transposed_values):
    pair_index = head_index // (H // KVH)
    head_query = lax.dynamic_slice_in_dim(queries, head_index * HEAD_SIZE, HEAD_SIZE, 1)
    head_key = lax.dynamic_slice_in_dim(transposed_keys, pair_index * HEAD_SIZE, HEAD_SIZE, 0)
    head_value = lax.dynamic_slice_in_dim(transposed_values, pair_index * HEAD_SIZE, HEAD_SIZE, 0)
    amount = jnp.where(head_index < H // 2, HALF, 0).astype(jnp.int32)
    head_query = jnp.roll(head_query, -amount, axis=0)
    head_key = jnp.roll(head_key, -amount, axis=1)
    head_value = jnp.roll(head_value, -amount, axis=1)
    group_count = SEQ_LEN // GROUP
    group_queries = head_query.reshape(group_count, GROUP, HEAD_SIZE)
    group_keys = jnp.transpose(head_key.reshape(HEAD_SIZE, group_count, GROUP), (1, 0, 2))
    group_values = jnp.transpose(head_value.reshape(HEAD_SIZE, group_count, GROUP), (1, 0, 2))
    context = lax.map(group_attend, (group_queries, group_keys, group_values))
    return jnp.roll(context.reshape(SEQ_LEN, HEAD_SIZE), amount, axis=0)

def reference(queries, transposed_keys, transposed_values, adapter_down_factor, adapter_up_factor, projection_output_gradient):

    def per_head(head_index):
        return one_head(head_index, queries, transposed_keys, transposed_values)
    contexts = lax.map(per_head, jnp.arange(H, dtype=jnp.int32))
    attention_result = jnp.transpose(contexts, (1, 0, 2)).reshape(SEQ_LEN, MODEL_WIDTH)
    adapter_activations = lax.dot_general(adapter_down_factor, attention_result, (((0,), (1,)), ((), ())), preferred_element_type=jnp.float32)
    rank_gradient_rows = lax.dot_general(adapter_up_factor, projection_output_gradient, (((1,), (1,)), ((), ())), preferred_element_type=jnp.float32).astype(jnp.bfloat16)
    down_factor_gradient = adapter_scale * lax.dot_general(attention_result, rank_gradient_rows, (((0,), (1,)), ((), ())), preferred_element_type=jnp.float32)
    rounded_activations = adapter_activations.astype(jnp.bfloat16)
    up_factor_gradient = adapter_scale * jnp.dot(rounded_activations, projection_output_gradient, preferred_element_type=jnp.float32)
    return (adapter_activations, down_factor_gradient, up_factor_gradient)
```

```python
import functools
import math

import jax
import jax.numpy as jnp
from jax import lax
from jax.experimental import pallas as pl
from jax.experimental.pallas import tpu as pltpu
from jax.sharding import PartitionSpec as P

neg_big = -1e30
adapter_scale = 2.0
head_size = 128
block = 512
sum_type = jnp.bfloat16
NT = (((1,), (1,)), ((), ()))
TN = (((0,), (0,)), ((), ()))


def pieces_of(rows, columns, count):
    across = min(count, columns // 128)
    down = count // across
    return rows // down, columns // across, across


def kernel(
    n_seq,
    n_head,
    q_hbm,
    k_hbm,
    v_hbm,
    down_ref,
    up_ref,
    grad_hbm,
    act_out,
    down_out,
    up_out,
    q_ref,
    grad_ref,
    k_ref,
    v_ref,
    kt_ref,
    attn_ref,
    back_pair,
    back_pair_in,
    back_send,
    back_in,
    back_all,
    back_ref,
    act_pair,
    act_pair_in,
    act_send,
    act_in,
    act_all,
    low_ref,
    seq_send,
    seq_in,
    seq_all,
    local_sem,
    kv_send,
    kv_in,
    pair_send_sem,
    pair_in_sem,
    rs_send_sem,
    rs_in_sem,
    ag_send_sem,
    ag_in_sem,
    seq_send_sem,
    seq_in_sem,
):
    me_s, me_h = lax.axis_index("seq"), lax.axis_index("head")
    n_chip = n_head // 2
    chip, core = me_h // 2, me_h % 2
    partner = {"head": me_h + 1 - 2 * core}
    sh = 1 - me_h // (n_head // 2)
    length = q_ref.shape[0]
    half = length // 2
    n_local = q_ref.shape[1] // head_size
    rank = up_ref.shape[0]
    mid = rank // 2
    own = k_hbm.shape[0]
    n_block = length // block
    pr, pc, across = pieces_of(mid, block, n_chip)
    sr, sc, s_across = pieces_of(rank, block, n_seq)

    def piece(value, index):
        r, c = (index // across) * pr, (index % across) * pc
        return value[r : r + pr, c : c + pc]

    def remote(src, dst, send, recv, device):
        copy = pltpu.make_async_remote_copy(
            src_ref=src,
            dst_ref=dst,
            send_sem=send,
            recv_sem=recv,
            device_id=device,
            device_id_type=pl.DeviceIdType.MESH,
        )
        copy.start()
        return copy

    def settle(ref, sem):
        pltpu.make_async_copy(ref, ref, sem).wait()

    barrier = pltpu.get_barrier_semaphore()
    for step in range(1, n_head):
        pl.semaphore_signal(
            barrier,
            inc=1,
            device_id={"head": lax.rem(me_h + step, n_head)},
            device_id_type=pl.DeviceIdType.MESH,
        )
    for step in range(1, n_seq):
        pl.semaphore_signal(
            barrier,
            inc=1,
            device_id={"seq": lax.rem(me_s + step, n_seq)},
            device_id_type=pl.DeviceIdType.MESH,
        )

    own_rows = pl.ds(pl.multiple_of(core * own, own), own)
    grad_copy = pltpu.make_async_copy(grad_hbm, grad_ref, local_sem.at[0])
    k_copy = pltpu.make_async_copy(k_hbm, k_ref.at[own_rows, pl.ds(half, length)], local_sem.at[1])
    v_copy = pltpu.make_async_copy(v_hbm, v_ref.at[own_rows, pl.ds(half, length)], local_sem.at[2])
    q_copy = pltpu.make_async_copy(q_hbm, q_ref, local_sem.at[3])
    for copy in (grad_copy, k_copy, v_copy, q_copy):
        copy.start()

    grad_copy.wait()
    for b in range(n_block):
        part = lax.dot_general(
            up_ref[...],
            grad_ref[b * block : (b + 1) * block, :],
            NT,
            preferred_element_type=jnp.float32,
        )
        back_pair[0, b] = part[:mid]
        back_pair[1, b] = part[mid:]
    pl.semaphore_wait(barrier, n_head + n_seq - 2)

    kv_copies = []
    for i, (src, dst) in enumerate(((k_hbm, k_ref), (v_hbm, v_ref))):
        kv_copies.append(
            remote(
                src,
                dst.at[own_rows, pl.ds(half, length)],
                kv_send.at[i],
                kv_in.at[i],
                partner,
            )
        )

    def tail_copy(i, src, dst):
        return pltpu.make_async_remote_copy(
            src_ref=src.at[:, pl.ds(half, half)],
            dst_ref=dst.at[own_rows, pl.ds(0, half)],
            send_sem=kv_send.at[2 + i],
            recv_sem=kv_in.at[2 + i],
            device_id={"seq": lax.rem(me_s + 1, n_seq)},
            device_id_type=pl.DeviceIdType.MESH,
        )

    def forward_copy(i, ref):
        return pltpu.make_async_remote_copy(
            src_ref=ref.at[own_rows, pl.ds(0, half)],
            dst_ref=ref.at[own_rows, pl.ds(0, half)],
            send_sem=kv_send.at[4 + i],
            recv_sem=kv_in.at[4 + i],
            device_id=partner,
            device_id_type=pl.DeviceIdType.MESH,
        )

    tails = [tail_copy(0, k_hbm, k_ref), tail_copy(1, v_hbm, v_ref)]
    forwards = [forward_copy(0, k_ref), forward_copy(1, v_ref)]

    @pl.when(sh == 1)
    def _():
        for copy in tails:
            copy.start()

    back_pair_copy = remote(
        back_pair.at[1 - core],
        back_pair_in,
        pair_send_sem.at[n_block],
        pair_in_sem.at[n_block],
        partner,
    )

    for copy in (k_copy, v_copy, q_copy):
        copy.wait()
    kv_copies[0].wait_recv()
    kv_copies[1].wait_recv()
    for c in range(half, half + length, block):
        kt_ref[c : c + block, :] = k_ref[:, c : c + block].T

    def peers():
        for step in range(1, n_chip):
            yield lax.rem(chip + step, n_chip)

    def back_scatter():
        back_pair_copy.wait_recv()
        for b in range(n_block):
            total = back_pair[core, b] + back_pair_in[b]
            for p in range(n_chip):
                back_send[p, b] = piece(total, p).astype(sum_type)
        back_in[chip] = back_send[chip]
        for peer in peers():
            remote(
                back_send.at[peer],
                back_in.at[chip],
                rs_send_sem.at[n_block],
                rs_in_sem.at[n_block],
                {"head": peer * 2 + core},
            )

    def gather_send(buffer, index):
        for step in range(1, n_head):
            remote(
                buffer.at[me_h],
                buffer.at[me_h],
                ag_send_sem.at[index],
                ag_in_sem.at[index],
                {"head": lax.rem(me_h + step, n_head)},
            )

    def back_gather():
        settle(back_in.at[pl.ds(0, n_chip - 1)], rs_in_sem.at[n_block])
        total = back_in[0].astype(jnp.float32)
        for p in range(1, n_chip):
            total = total + back_in[p].astype(jnp.float32)
        back_all[me_h] = total.astype(jnp.bfloat16)
        gather_send(back_all, 2)

    def place(d):
        r = (d % 2) * mid + ((d // 2) // across) * pr
        c = ((d // 2) % across) * pc
        return r, c

    def back_finish():
        settle(back_all.at[pl.ds(0, n_head - 1)], ag_in_sem.at[2])
        for d in range(n_head):
            r, c = place(d)
            for b in range(n_block):
                back_ref[r : r + pr, b * block + c : b * block + c + pc] = back_all[d, b]

    def block_of(n):
        return lax.rem(n - 1 + sh * (n_block // 2), n_block)

    def act_part(n):
        b = block_of(n)
        columns = pl.ds(pl.multiple_of(b * block, block), block)
        part = lax.dot_general(
            down_ref[...], attn_ref[:, columns], TN, preferred_element_type=jnp.float32
        )
        act_pair[n - 1, 0] = part[:mid]
        act_pair[n - 1, 1] = part[mid:]
        return remote(
            act_pair.at[n - 1, 1 - core],
            act_pair_in.at[n - 1],
            pair_send_sem.at[n - 1],
            pair_in_sem.at[n - 1],
            partner,
        )

    def act_scatter(n, copy):
        b = block_of(n)
        copy.wait_recv()
        total = act_pair[n - 1, core] + act_pair_in[n - 1]
        for p in range(n_chip):
            act_send[n - 1, p] = piece(total, p).astype(sum_type)
        act_in[b, chip] = act_send[n - 1, chip]
        for peer in peers():
            remote(
                act_send.at[n - 1, peer],
                act_in.at[b, chip],
                rs_send_sem.at[n - 1],
                rs_in_sem.at[b],
                {"head": peer * 2 + core},
            )

    def act_gather(odd):
        for i, b in enumerate(range(odd, n_block, 2)):
            settle(act_in.at[b, pl.ds(0, n_chip - 1)], rs_in_sem.at[b])
            total = act_in[b, 0].astype(jnp.float32)
            for p in range(1, n_chip):
                total = total + act_in[b, p].astype(jnp.float32)
            act_all[odd, me_h, i] = total.astype(jnp.bfloat16)
        gather_send(act_all.at[odd], odd)

    def act_finish(odd):
        settle(act_all.at[odd, pl.ds(0, n_head - 1)], ag_in_sem.at[odd])
        for d in range(n_head):
            r, c = place(d)
            for i, b in enumerate(range(odd, n_block, 2)):
                value = act_all[odd, d, i]
                low_ref[r : r + pr, b * block + c : b * block + c + pc] = value
                act_out[r : r + pr, b * block + c : b * block + c + pc] = value.astype(jnp.float32)

    def up_part(odd):
        total = None
        for b in range(odd, n_block, 2):
            term = jnp.dot(
                low_ref[:, b * block : (b + 1) * block],
                grad_ref[b * block : (b + 1) * block, :],
                preferred_element_type=jnp.float32,
            )
            total = term if total is None else total + term
        return total

    sub = block // 2
    factor = math.log2(math.e) / math.sqrt(head_size)

    def attend(n, hooks):
        b = block_of(n)
        shifted_start = length if n <= n_block // 2 else 0
        start = pl.multiple_of(half + sh * (shifted_start - half), half)

        def body(h, carry):
            for at, hook in hooks:
                pl.when(h == at)(hook)
            columns = pl.ds(pl.multiple_of(h * head_size, head_size), head_size)
            for r in range(2):
                rows = pl.ds(pl.multiple_of(b * block + r * sub, sub), sub)
                query = q_ref[rows, columns]
                count = (n - 1) * 2 + r + 1
                scores = []
                for j in range(count):
                    keys = kt_ref[pl.ds(pl.multiple_of(start + j * sub, sub), sub), :]
                    score = lax.dot_general(keys, query, NT, preferred_element_type=jnp.float32)
                    if j == count - 1:
                        key_index = lax.broadcasted_iota(jnp.int32, score.shape, 0)
                        row_index = lax.broadcasted_iota(jnp.int32, score.shape, 1)
                        score = jnp.where(key_index <= row_index, score, neg_big)
                    scores.append(score)
                top = jnp.max(scores[0], axis=0, keepdims=True)
                for score in scores[1:]:
                    top = jnp.maximum(top, jnp.max(score, axis=0, keepdims=True))
                total, context = None, None
                for j in range(count):
                    weights = jnp.exp2((scores[j] - top) * factor)
                    row_sum = jnp.sum(weights, axis=0, keepdims=True)
                    values = v_ref[:, pl.ds(pl.multiple_of(start + j * sub, sub), sub)]
                    term = jnp.dot(
                        values, weights.astype(jnp.bfloat16), preferred_element_type=jnp.float32
                    )
                    total = row_sum if total is None else total + row_sum
                    context = term if context is None else context + term
                attn_ref[columns, rows] = (context * (1.0 / total)).astype(jnp.bfloat16)
            return carry

        lax.fori_loop(0, n_local, body, 0)

    pairs = {}
    attend(2, [(1, back_scatter)])
    pairs[2] = act_part(2)

    @pl.when(sh == 1)
    def _():
        for tail, forward in zip(tails, forwards):
            tail.wait_recv()
            forward.start()

    attend(1, [])
    pairs[1] = act_part(1)

    @pl.when(sh == 1)
    def _():
        for copy in forwards:
            copy.wait_recv()
        for c in range(0, half, block):
            kt_ref[c : c + block, :] = k_ref[:, c : c + block].T

    def early():
        act_scatter(2, pairs[2])
        act_scatter(1, pairs[1])
        back_gather()

    attend(4, [(1, early)])
    pairs[4] = act_part(4)

    def late():
        act_scatter(4, pairs[4])
        back_finish()

    attend(3, [(1, late), (3, functools.partial(act_gather, 1))])
    pairs[3] = act_part(3)

    def seq_scatter(kind, value):
        for p in range(n_seq):
            r, c = (p // s_across) * sr, (p % s_across) * sc
            seq_send[kind, p] = value[r : r + sr, c : c + sc]
        seq_in[kind, me_s] = seq_send[kind, me_s]
        for step in range(1, n_seq):
            peer = lax.rem(me_s + step, n_seq)
            remote(
                seq_send.at[kind, peer],
                seq_in.at[kind, me_s],
                seq_send_sem.at[kind, 0],
                seq_in_sem.at[kind, 0],
                {"seq": peer},
            )

    def seq_gather(kind):
        settle(seq_in.at[kind, pl.ds(0, n_seq - 1)], seq_in_sem.at[kind, 0])
        total = seq_in[kind, 0]
        for p in range(1, n_seq):
            total = total + seq_in[kind, p]
        seq_all[kind, me_s] = total * adapter_scale
        for step in range(1, n_seq):
            remote(
                seq_all.at[kind, me_s],
                seq_all.at[kind, me_s],
                seq_send_sem.at[kind, 1],
                seq_in_sem.at[kind, 1],
                {"seq": lax.rem(me_s + step, n_seq)},
            )

    act_finish(1)
    up_total = up_part(1)
    act_scatter(3, pairs[3])
    seq_scatter(
        0,
        lax.dot_general(back_ref[...], attn_ref[...], NT, preferred_element_type=jnp.float32),
    )
    act_gather(0)
    seq_gather(0)
    act_finish(0)
    seq_scatter(1, up_total + up_part(0))

    settle(seq_all.at[0, pl.ds(0, n_seq - 1)], seq_in_sem.at[0, 1])
    for p in range(n_seq):
        r, c = (p // s_across) * sr, (p % s_across) * sc
        down_out[c : c + sc, r : r + sr] = seq_all[0, p].T
    seq_gather(1)
    settle(seq_all.at[1, pl.ds(0, n_seq - 1)], seq_in_sem.at[1, 1])
    for p in range(n_seq):
        r, c = (p // s_across) * sr, (p % s_across) * sc
        up_out[r : r + sr, c : c + sc] = seq_all[1, p]

    kv_copies[0].wait_send()
    kv_copies[1].wait_send()
    back_pair_copy.wait_send()
    for n in range(1, n_block + 1):
        pairs[n].wait_send()
        settle(act_send.at[n - 1, pl.ds(0, n_chip - 1)], rs_send_sem.at[n - 1])
    settle(back_send.at[pl.ds(0, n_chip - 1)], rs_send_sem.at[n_block])
    settle(act_all.at[0, pl.ds(0, n_head - 1)], ag_send_sem.at[0])
    settle(act_all.at[1, pl.ds(0, n_head - 1)], ag_send_sem.at[1])
    settle(back_all.at[pl.ds(0, n_head - 1)], ag_send_sem.at[2])
    for kind in range(2):
        settle(seq_send.at[kind, pl.ds(0, n_seq - 1)], seq_send_sem.at[kind, 0])
        settle(seq_all.at[kind, pl.ds(0, n_seq - 1)], seq_send_sem.at[kind, 1])

    @pl.when(sh == 1)
    def _():
        for copy in tails + forwards:
            copy.wait_send()


def solution(mesh):
    n_seq, n_head = mesh.shape["seq"], mesh.shape["head"]
    n_chip = n_head // 2
    in_specs = (
        P("seq", "head"),
        P("head", "seq"),
        P("head", "seq"),
        P("head", None),
        P(None, "head"),
        P("seq", "head"),
    )
    out_specs = (P(None, "seq"), P("head", None), P(None, "head"))

    def on_device(queries, keys, values, down_factor, up_factor, gradient):
        length, width = queries.shape
        own = keys.shape[0]
        rank = up_factor.shape[0]
        n_block = length // block
        joined = length + length // 2
        pr, pc, _ = pieces_of(rank // 2, block, n_chip)
        sr, sc, _ = pieces_of(rank, block, n_seq)
        f32, b16 = jnp.float32, jnp.bfloat16
        dma = pltpu.SemaphoreType.DMA
        anywhere = pl.BlockSpec(memory_space=pl.ANY)
        vmem = pl.BlockSpec(memory_space=pltpu.VMEM)
        return pl.pallas_call(
            functools.partial(kernel, n_seq, n_head),
            out_shape=(
                jax.ShapeDtypeStruct((rank, length), f32),
                jax.ShapeDtypeStruct((width, rank), f32),
                jax.ShapeDtypeStruct((rank, width), f32),
            ),
            in_specs=[anywhere, anywhere, anywhere, vmem, vmem, anywhere],
            out_specs=(vmem, vmem, vmem),
            scratch_shapes=[
                pltpu.VMEM((length, width), b16),
                pltpu.VMEM((length, width), b16),
                pltpu.VMEM((2 * own, joined), b16),
                pltpu.VMEM((2 * own, joined), b16),
                pltpu.VMEM((joined, 2 * own), b16),
                pltpu.VMEM((width, length), b16),
                pltpu.VMEM((2, n_block, rank // 2, block), f32),
                pltpu.VMEM((n_block, rank // 2, block), f32),
                pltpu.VMEM((n_chip, n_block, pr, pc), sum_type),
                pltpu.VMEM((n_chip, n_block, pr, pc), sum_type),
                pltpu.VMEM((n_head, n_block, pr, pc), b16),
                pltpu.VMEM((rank, length), b16),
                pltpu.VMEM((n_block, 2, rank // 2, block), f32),
                pltpu.VMEM((n_block, rank // 2, block), f32),
                pltpu.VMEM((n_block, n_chip, pr, pc), sum_type),
                pltpu.VMEM((n_block, n_chip, pr, pc), sum_type),
                pltpu.VMEM((2, n_head, n_block // 2, pr, pc), b16),
                pltpu.VMEM((rank, length), b16),
                pltpu.VMEM((2, n_seq, sr, sc), f32),
                pltpu.VMEM((2, n_seq, sr, sc), f32),
                pltpu.VMEM((2, n_seq, sr, sc), f32),
                dma((4,)),
                dma((6,)),
                dma((6,)),
                dma((n_block + 1,)),
                dma((n_block + 1,)),
                dma((n_block + 1,)),
                dma((n_block + 1,)),
                dma((3,)),
                dma((3,)),
                dma((2, 2)),
                dma((2, 2)),
            ],
            compiler_params=pltpu.CompilerParams(
                collective_id=0, has_side_effects=True, vmem_limit_bytes=56 * 2**20
            ),
            cost_estimate=pl.CostEstimate(
                flops=6 * 10**9, bytes_accessed=8 * 2**20, transcendentals=10**7
            ),
        )(queries, keys, values, down_factor, up_factor, gradient)

    return jax.shard_map(
        on_device, mesh=mesh, in_specs=in_specs, out_specs=out_specs, check_vma=False
    )
```

```python
import functools
import math

import jax
import jax.numpy as jnp
from jax import lax
from jax.experimental import pallas as pl
from jax.experimental.pallas import tpu as pltpu
from jax.sharding import PartitionSpec as P

neg_big = -1e30
adapter_scale = 2.0
head_size = 128
block = 512
sum_type = jnp.bfloat16
NT = (((1,), (1,)), ((), ()))


def pieces_of(rows, columns, count):
    across = min(count, columns // 128)
    down = count // across
    return rows // down, columns // across, across


def kernel(
    n_seq,
    n_head,
    q_hbm,
    k_hbm,
    v_hbm,
    down_ref,
    up_ref,
    grad_hbm,
    low_ref,
    down_out,
    up_out,
    q_ref,
    grad_ref,
    k_ref,
    v_ref,
    vt_ref,
    attn_ref,
    back_pair,
    back_pair_in,
    back_send,
    back_in,
    back_all,
    back_ref,
    act_pair,
    act_pair_in,
    act_send,
    act_in,
    act_all,
    seq_send,
    seq_in,
    seq_all,
    local_sem,
    kv_send,
    kv_in,
    pair_send_sem,
    pair_in_sem,
    rs_send_sem,
    rs_in_sem,
    ag_send_sem,
    ag_in_sem,
    seq_send_sem,
    seq_in_sem,
):
    me_s, me_h = lax.axis_index("seq"), lax.axis_index("head")
    n_chip = n_head // 2
    chip, core = me_h // 2, me_h % 2
    partner = {"head": me_h + 1 - 2 * core}
    sh = 1 - me_h // (n_head // 2)
    length = q_ref.shape[0]
    half = length // 2
    n_local = q_ref.shape[1] // head_size
    rank = up_ref.shape[0]
    mid = rank // 2
    own = k_hbm.shape[0]
    n_block = length // block
    pr, pc, across = pieces_of(mid, block, n_chip)
    sr, sc, s_across = pieces_of(rank, block, n_seq)

    def piece(value, index):
        r, c = (index // across) * pr, (index % across) * pc
        return value[r : r + pr, c : c + pc]

    def remote(src, dst, send, recv, device):
        copy = pltpu.make_async_remote_copy(
            src_ref=src,
            dst_ref=dst,
            send_sem=send,
            recv_sem=recv,
            device_id=device,
            device_id_type=pl.DeviceIdType.MESH,
        )
        copy.start()
        return copy

    def settle(ref, sem):
        pltpu.make_async_copy(ref, ref, sem).wait()

    barrier = pltpu.get_barrier_semaphore()
    for step in range(1, n_head):
        pl.semaphore_signal(
            barrier,
            inc=1,
            device_id={"head": lax.rem(me_h + step, n_head)},
            device_id_type=pl.DeviceIdType.MESH,
        )
    for step in range(1, n_seq):
        pl.semaphore_signal(
            barrier,
            inc=1,
            device_id={"seq": lax.rem(me_s + step, n_seq)},
            device_id_type=pl.DeviceIdType.MESH,
        )

    own_rows = pl.ds(pl.multiple_of(core * own, own), own)
    grad_copy = pltpu.make_async_copy(grad_hbm, grad_ref, local_sem.at[0])
    k_copy = pltpu.make_async_copy(k_hbm, k_ref.at[own_rows, pl.ds(half, length)], local_sem.at[1])
    v_copy = pltpu.make_async_copy(v_hbm, v_ref.at[own_rows, pl.ds(half, length)], local_sem.at[2])
    q_copy = pltpu.make_async_copy(q_hbm, q_ref, local_sem.at[3])
    for copy in (grad_copy, k_copy, v_copy, q_copy):
        copy.start()

    grad_copy.wait()
    for b in range(n_block):
        part = lax.dot_general(
            up_ref[...],
            grad_ref[b * block : (b + 1) * block, :],
            NT,
            preferred_element_type=jnp.float32,
        )
        back_pair[0, b] = part[:mid]
        back_pair[1, b] = part[mid:]
    pl.semaphore_wait(barrier, n_head + n_seq - 2)

    kv_copies = []
    for i, (src, dst) in enumerate(((k_hbm, k_ref), (v_hbm, v_ref))):
        kv_copies.append(
            remote(
                src,
                dst.at[own_rows, pl.ds(half, length)],
                kv_send.at[i],
                kv_in.at[i],
                partner,
            )
        )

    def tail_copy(i, src, dst):
        return pltpu.make_async_remote_copy(
            src_ref=src.at[:, pl.ds(half, half)],
            dst_ref=dst.at[own_rows, pl.ds(0, half)],
            send_sem=kv_send.at[2 + i],
            recv_sem=kv_in.at[2 + i],
            device_id={"seq": lax.rem(me_s + 1, n_seq)},
            device_id_type=pl.DeviceIdType.MESH,
        )

    def forward_copy(i, ref):
        return pltpu.make_async_remote_copy(
            src_ref=ref.at[own_rows, pl.ds(0, half)],
            dst_ref=ref.at[own_rows, pl.ds(0, half)],
            send_sem=kv_send.at[4 + i],
            recv_sem=kv_in.at[4 + i],
            device_id=partner,
            device_id_type=pl.DeviceIdType.MESH,
        )

    tails = [tail_copy(0, k_hbm, k_ref), tail_copy(1, v_hbm, v_ref)]
    forwards = [forward_copy(0, k_ref), forward_copy(1, v_ref)]

    @pl.when(sh == 1)
    def _():
        for copy in tails:
            copy.start()

    back_pair_copy = remote(
        back_pair.at[1 - core],
        back_pair_in,
        pair_send_sem.at[n_block],
        pair_in_sem.at[n_block],
        partner,
    )

    for copy in (k_copy, v_copy, q_copy):
        copy.wait()
    kv_copies[0].wait_recv()
    kv_copies[1].wait_recv()
    for c in range(half, half + length, block):
        vt_ref[c : c + block, :] = v_ref[:, c : c + block].T

    def peers():
        for step in range(1, n_chip):
            yield lax.rem(chip + step, n_chip)

    def back_scatter():
        back_pair_copy.wait_recv()
        for b in range(n_block):
            total = back_pair[core, b] + back_pair_in[b]
            for p in range(n_chip):
                back_send[p, b] = piece(total, p).astype(sum_type)
        back_in[chip] = back_send[chip]
        for peer in peers():
            remote(
                back_send.at[peer],
                back_in.at[chip],
                rs_send_sem.at[n_block],
                rs_in_sem.at[n_block],
                {"head": peer * 2 + core},
            )

    def gather_send(buffer, index):
        for step in range(1, n_head):
            remote(
                buffer.at[me_h],
                buffer.at[me_h],
                ag_send_sem.at[index],
                ag_in_sem.at[index],
                {"head": lax.rem(me_h + step, n_head)},
            )

    def back_gather():
        settle(back_in.at[pl.ds(0, n_chip - 1)], rs_in_sem.at[n_block])
        total = back_in[0].astype(jnp.float32)
        for p in range(1, n_chip):
            total = total + back_in[p].astype(jnp.float32)
        back_all[me_h] = total.astype(jnp.bfloat16)
        gather_send(back_all, 2)

    def place(d):
        r = (d % 2) * mid + ((d // 2) // across) * pr
        c = ((d // 2) % across) * pc
        return r, c

    def back_finish():
        settle(back_all.at[pl.ds(0, n_head - 1)], ag_in_sem.at[2])
        for d in range(n_head):
            r, c = place(d)
            for b in range(n_block):
                back_ref[r : r + pr, b * block + c : b * block + c + pc] = back_all[d, b]

    def block_of(n):
        return lax.rem(n - 1 + sh * (n_block // 2), n_block)

    def act_part(n):
        b = block_of(n)
        rows = pl.ds(pl.multiple_of(b * block, block), block)
        part = lax.dot_general(
            down_ref[...], attn_ref[rows, :], NT, preferred_element_type=jnp.float32
        )
        act_pair[n - 1, 0] = part[:mid]
        act_pair[n - 1, 1] = part[mid:]
        return remote(
            act_pair.at[n - 1, 1 - core],
            act_pair_in.at[n - 1],
            pair_send_sem.at[n - 1],
            pair_in_sem.at[n - 1],
            partner,
        )

    def act_scatter(n, copy):
        b = block_of(n)
        copy.wait_recv()
        total = act_pair[n - 1, core] + act_pair_in[n - 1]
        for p in range(n_chip):
            act_send[n - 1, p] = piece(total, p).astype(sum_type)
        act_in[b, chip] = act_send[n - 1, chip]
        for peer in peers():
            remote(
                act_send.at[n - 1, peer],
                act_in.at[b, chip],
                rs_send_sem.at[n - 1],
                rs_in_sem.at[b],
                {"head": peer * 2 + core},
            )

    def act_gather(odd):
        for i, b in enumerate(range(odd, n_block, 2)):
            settle(act_in.at[b, pl.ds(0, n_chip - 1)], rs_in_sem.at[b])
            total = act_in[b, 0].astype(jnp.float32)
            for p in range(1, n_chip):
                total = total + act_in[b, p].astype(jnp.float32)
            act_all[odd, me_h, i] = total.astype(jnp.bfloat16)
        gather_send(act_all.at[odd], odd)

    def act_finish(odd):
        settle(act_all.at[odd, pl.ds(0, n_head - 1)], ag_in_sem.at[odd])
        for d in range(n_head):
            r, c = place(d)
            for i, b in enumerate(range(odd, n_block, 2)):
                value = act_all[odd, d, i]
                low_ref[r : r + pr, b * block + c : b * block + c + pc] = value

    def up_part(odd):
        total = None
        for b in range(odd, n_block, 2):
            term = jnp.dot(
                low_ref[:, b * block : (b + 1) * block],
                grad_ref[b * block : (b + 1) * block, :],
                preferred_element_type=jnp.float32,
            )
            total = term if total is None else total + term
        return total

    sub = block // 2
    factor = math.log2(math.e) / math.sqrt(head_size)

    def attend(n, hooks):
        b = block_of(n)
        shifted_start = length if n <= n_block // 2 else 0
        start = pl.multiple_of(half + sh * (shifted_start - half), half)

        def body(h, carry):
            for at, hook in hooks:
                pl.when(h == at)(hook)
            columns = pl.ds(pl.multiple_of(h * head_size, head_size), head_size)
            for r in range(2):
                rows = pl.ds(pl.multiple_of(b * block + r * sub, sub), sub)
                count = ((n - 1) * 2 + r + 1) * sub
                keys = pl.ds(start, count)
                scores = jnp.dot(
                    q_ref[rows, columns], k_ref[:, keys], preferred_element_type=jnp.float32
                )
                last = scores[:, count - sub :]
                row_index = lax.broadcasted_iota(jnp.int32, last.shape, 0)
                key_index = lax.broadcasted_iota(jnp.int32, last.shape, 1)
                last = jnp.where(key_index <= row_index, last, neg_big)
                if count > sub:
                    scores = jnp.concatenate([scores[:, : count - sub], last], axis=1)
                else:
                    scores = last
                top = jnp.max(scores, axis=1, keepdims=True)
                weights = jnp.exp2((scores - top) * factor)
                total = jnp.sum(weights, axis=1, keepdims=True)
                context = jnp.dot(
                    weights.astype(jnp.bfloat16), vt_ref[keys, :], preferred_element_type=jnp.float32
                )
                attn_ref[rows, columns] = (context * (1.0 / total)).astype(jnp.bfloat16)
            return carry

        lax.fori_loop(0, n_local, body, 0)

    pairs = {}
    attend(2, [(1, back_scatter)])
    pairs[2] = act_part(2)

    @pl.when(sh == 1)
    def _():
        for tail, forward in zip(tails, forwards):
            tail.wait_recv()
            forward.start()

    attend(1, [])
    pairs[1] = act_part(1)

    @pl.when(sh == 1)
    def _():
        for copy in forwards:
            copy.wait_recv()
        for c in range(0, half, block):
            vt_ref[c : c + block, :] = v_ref[:, c : c + block].T

    def early():
        act_scatter(2, pairs[2])
        act_scatter(1, pairs[1])
        back_gather()

    attend(4, [(1, early)])
    pairs[4] = act_part(4)

    def late():
        act_scatter(4, pairs[4])
        back_finish()

    attend(3, [(1, late), (3, functools.partial(act_gather, 1))])
    pairs[3] = act_part(3)

    def seq_scatter(kind, value):
        for p in range(n_seq):
            r, c = (p // s_across) * sr, (p % s_across) * sc
            seq_send[kind, p] = value[r : r + sr, c : c + sc]
        seq_in[kind, me_s] = seq_send[kind, me_s]
        for step in range(1, n_seq):
            peer = lax.rem(me_s + step, n_seq)
            remote(
                seq_send.at[kind, peer],
                seq_in.at[kind, me_s],
                seq_send_sem.at[kind, 0],
                seq_in_sem.at[kind, 0],
                {"seq": peer},
            )

    def seq_gather(kind):
        settle(seq_in.at[kind, pl.ds(0, n_seq - 1)], seq_in_sem.at[kind, 0])
        total = seq_in[kind, 0]
        for p in range(1, n_seq):
            total = total + seq_in[kind, p]
        seq_all[kind, me_s] = total * adapter_scale
        for step in range(1, n_seq):
            remote(
                seq_all.at[kind, me_s],
                seq_all.at[kind, me_s],
                seq_send_sem.at[kind, 1],
                seq_in_sem.at[kind, 1],
                {"seq": lax.rem(me_s + step, n_seq)},
            )

    act_finish(1)
    up_total = up_part(1)
    act_scatter(3, pairs[3])
    seq_scatter(
        0,
        jnp.dot(back_ref[...], attn_ref[...], preferred_element_type=jnp.float32),
    )
    act_gather(0)
    seq_gather(0)
    act_finish(0)
    seq_scatter(1, up_total + up_part(0))

    settle(seq_all.at[0, pl.ds(0, n_seq - 1)], seq_in_sem.at[0, 1])
    for p in range(n_seq):
        r, c = (p // s_across) * sr, (p % s_across) * sc
        down_out[r : r + sr, c : c + sc] = seq_all[0, p]
    seq_gather(1)
    settle(seq_all.at[1, pl.ds(0, n_seq - 1)], seq_in_sem.at[1, 1])
    for p in range(n_seq):
        r, c = (p // s_across) * sr, (p % s_across) * sc
        up_out[r : r + sr, c : c + sc] = seq_all[1, p]

    kv_copies[0].wait_send()
    kv_copies[1].wait_send()
    back_pair_copy.wait_send()
    for n in range(1, n_block + 1):
        pairs[n].wait_send()
        settle(act_send.at[n - 1, pl.ds(0, n_chip - 1)], rs_send_sem.at[n - 1])
    settle(back_send.at[pl.ds(0, n_chip - 1)], rs_send_sem.at[n_block])
    settle(act_all.at[0, pl.ds(0, n_head - 1)], ag_send_sem.at[0])
    settle(act_all.at[1, pl.ds(0, n_head - 1)], ag_send_sem.at[1])
    settle(back_all.at[pl.ds(0, n_head - 1)], ag_send_sem.at[2])
    for kind in range(2):
        settle(seq_send.at[kind, pl.ds(0, n_seq - 1)], seq_send_sem.at[kind, 0])
        settle(seq_all.at[kind, pl.ds(0, n_seq - 1)], seq_send_sem.at[kind, 1])

    @pl.when(sh == 1)
    def _():
        for copy in tails + forwards:
            copy.wait_send()


def finish(low_ref, down_ref, up_ref, act_out, down_out, up_out):
    act_out[...] = low_ref[...].astype(jnp.float32)
    down_out[...] = down_ref[...]
    up_out[...] = up_ref[...]


def solution(mesh):
    n_seq, n_head = mesh.shape["seq"], mesh.shape["head"]
    n_chip = n_head // 2
    in_specs = (
        P("seq", "head"),
        P("head", "seq"),
        P("head", "seq"),
        P("head", None),
        P(None, "head"),
        P("seq", "head"),
    )
    out_specs = (P(None, "seq"), P("head", None), P(None, "head"))

    def on_device(queries, keys, values, down_factor, up_factor, gradient):
        length, width = queries.shape
        own = keys.shape[0]
        rank = up_factor.shape[0]
        n_block = length // block
        joined = length + length // 2
        pr, pc, _ = pieces_of(rank // 2, block, n_chip)
        sr, sc, _ = pieces_of(rank, block, n_seq)
        f32, b16 = jnp.float32, jnp.bfloat16
        dma = pltpu.SemaphoreType.DMA
        anywhere = pl.BlockSpec(memory_space=pl.ANY)
        vmem = pl.BlockSpec(memory_space=pltpu.VMEM)
        low, down, up = pl.pallas_call(
            functools.partial(kernel, n_seq, n_head),
            out_shape=(
                jax.ShapeDtypeStruct((rank, length), b16),
                jax.ShapeDtypeStruct((rank, width), f32),
                jax.ShapeDtypeStruct((rank, width), f32),
            ),
            in_specs=[anywhere, anywhere, anywhere, vmem, vmem, anywhere],
            out_specs=(vmem, vmem, vmem),
            scratch_shapes=[
                pltpu.VMEM((length, width), b16),
                pltpu.VMEM((length, width), b16),
                pltpu.VMEM((2 * own, joined), b16),
                pltpu.VMEM((2 * own, joined), b16),
                pltpu.VMEM((joined, 2 * own), b16),
                pltpu.VMEM((length, width), b16),
                pltpu.VMEM((2, n_block, rank // 2, block), f32),
                pltpu.VMEM((n_block, rank // 2, block), f32),
                pltpu.VMEM((n_chip, n_block, pr, pc), sum_type),
                pltpu.VMEM((n_chip, n_block, pr, pc), sum_type),
                pltpu.VMEM((n_head, n_block, pr, pc), b16),
                pltpu.VMEM((rank, length), b16),
                pltpu.VMEM((n_block, 2, rank // 2, block), f32),
                pltpu.VMEM((n_block, rank // 2, block), f32),
                pltpu.VMEM((n_block, n_chip, pr, pc), sum_type),
                pltpu.VMEM((n_block, n_chip, pr, pc), sum_type),
                pltpu.VMEM((2, n_head, n_block // 2, pr, pc), b16),
                pltpu.VMEM((2, n_seq, sr, sc), f32),
                pltpu.VMEM((2, n_seq, sr, sc), f32),
                pltpu.VMEM((2, n_seq, sr, sc), f32),
                dma((4,)),
                dma((6,)),
                dma((6,)),
                dma((n_block + 1,)),
                dma((n_block + 1,)),
                dma((n_block + 1,)),
                dma((n_block + 1,)),
                dma((3,)),
                dma((3,)),
                dma((2, 2)),
                dma((2, 2)),
            ],
            compiler_params=pltpu.CompilerParams(
                collective_id=0, has_side_effects=True, vmem_limit_bytes=56 * 2**20
            ),
            cost_estimate=pl.CostEstimate(
                flops=6 * 10**9, bytes_accessed=8 * 2**20, transcendentals=10**7
            ),
        )(queries, keys, values, down_factor.T, up_factor, gradient)
        activations, down, up = pl.pallas_call(
            finish,
            out_shape=(
                jax.ShapeDtypeStruct((rank, length), f32),
                jax.ShapeDtypeStruct((rank, width), f32),
                jax.ShapeDtypeStruct((rank, width), f32),
            ),
            in_specs=[vmem, vmem, vmem],
            out_specs=(vmem, vmem, vmem),
        )(low, down, up)
        return activations, down.T, up

    return jax.shard_map(
        on_device, mesh=mesh, in_specs=in_specs, out_specs=out_specs, check_vma=False
    )
```

```python
import functools
import math

import jax
import jax.numpy as jnp
from jax import lax
from jax.experimental import pallas as pl
from jax.experimental.pallas import tpu as pltpu
from jax.sharding import PartitionSpec as P

neg_big = -1e30
adapter_scale = 2.0
head_size = 128
block = 512
sum_type = jnp.bfloat16
NT = (((1,), (1,)), ((), ()))


def pieces_of(rows, columns, count):
    across = min(count, columns // 128)
    down = count // across
    return rows // down, columns // across, across


def kernel(
    n_seq,
    n_head,
    q_hbm,
    k_hbm,
    v_hbm,
    down_ref,
    up_ref,
    grad_hbm,
    low_ref,
    down_out,
    up_out,
    q_ref,
    grad_ref,
    k_ref,
    v_ref,
    vt_ref,
    attn_ref,
    back_pair,
    back_pair_in,
    back_send,
    back_in,
    back_all,
    back_ref,
    act_pair,
    act_pair_in,
    act_send,
    act_in,
    act_all,
    last_send,
    last_in,
    s0_ref,
    s1_ref,
    seq_send,
    seq_in,
    seq_all,
    local_sem,
    kv_send,
    kv_in,
    pair_send_sem,
    pair_in_sem,
    rs_send_sem,
    rs_in_sem,
    ag_send_sem,
    ag_in_sem,
    seq_send_sem,
    seq_in_sem,
):
    me_s, me_h = lax.axis_index("seq"), lax.axis_index("head")
    n_chip = n_head // 2
    chip, core = me_h // 2, me_h % 2
    partner = {"head": me_h + 1 - 2 * core}
    sh = 1 - me_h // (n_head // 2)
    length = q_ref.shape[0]
    half = length // 2
    n_local = q_ref.shape[1] // head_size
    rank = up_ref.shape[0]
    mid = rank // 2
    own = k_hbm.shape[0]
    n_block = length // block
    pr, pc, across = pieces_of(mid, block, n_chip)
    sr, sc, s_across = pieces_of(rank, block, n_seq)

    def piece(value, index):
        r, c = (index // across) * pr, (index % across) * pc
        return value[r : r + pr, c : c + pc]

    def remote(src, dst, send, recv, device):
        copy = pltpu.make_async_remote_copy(
            src_ref=src,
            dst_ref=dst,
            send_sem=send,
            recv_sem=recv,
            device_id=device,
            device_id_type=pl.DeviceIdType.MESH,
        )
        copy.start()
        return copy

    def settle(ref, sem):
        pltpu.make_async_copy(ref, ref, sem).wait()

    barrier = pltpu.get_barrier_semaphore()
    for step in range(1, n_head):
        pl.semaphore_signal(
            barrier,
            inc=1,
            device_id={"head": lax.rem(me_h + step, n_head)},
            device_id_type=pl.DeviceIdType.MESH,
        )
    for step in range(1, n_seq):
        pl.semaphore_signal(
            barrier,
            inc=1,
            device_id={"seq": lax.rem(me_s + step, n_seq)},
            device_id_type=pl.DeviceIdType.MESH,
        )

    own_rows = pl.ds(pl.multiple_of(core * own, own), own)
    grad_copy = pltpu.make_async_copy(grad_hbm, grad_ref, local_sem.at[0])
    k_copy = pltpu.make_async_copy(k_hbm, k_ref.at[own_rows, pl.ds(half, length)], local_sem.at[1])
    v_copy = pltpu.make_async_copy(v_hbm, v_ref.at[own_rows, pl.ds(half, length)], local_sem.at[2])
    q_copy = pltpu.make_async_copy(q_hbm, q_ref, local_sem.at[3])
    for copy in (grad_copy, k_copy, v_copy, q_copy):
        copy.start()

    pl.semaphore_wait(barrier, n_head + n_seq - 2)

    kv_copies = []
    for i, (src, dst) in enumerate(((k_hbm, k_ref), (v_hbm, v_ref))):
        kv_copies.append(
            remote(
                src,
                dst.at[own_rows, pl.ds(half, length)],
                kv_send.at[i],
                kv_in.at[i],
                partner,
            )
        )

    def tail_copy(i, src, dst):
        return pltpu.make_async_remote_copy(
            src_ref=src.at[:, pl.ds(half, half)],
            dst_ref=dst.at[own_rows, pl.ds(0, half)],
            send_sem=kv_send.at[2 + i],
            recv_sem=kv_in.at[2 + i],
            device_id={"seq": lax.rem(me_s + 1, n_seq)},
            device_id_type=pl.DeviceIdType.MESH,
        )

    def forward_copy(i, ref):
        return pltpu.make_async_remote_copy(
            src_ref=ref.at[own_rows, pl.ds(0, half)],
            dst_ref=ref.at[own_rows, pl.ds(0, half)],
            send_sem=kv_send.at[4 + i],
            recv_sem=kv_in.at[4 + i],
            device_id=partner,
            device_id_type=pl.DeviceIdType.MESH,
        )

    tails = [tail_copy(0, k_hbm, k_ref), tail_copy(1, v_hbm, v_ref)]
    forwards = [forward_copy(0, k_ref), forward_copy(1, v_ref)]

    @pl.when(sh == 1)
    def _():
        for copy in tails:
            copy.start()

    grad_copy.wait()
    for b in range(n_block):
        part = lax.dot_general(
            up_ref[...],
            grad_ref[b * block : (b + 1) * block, :],
            NT,
            preferred_element_type=jnp.float32,
        )
        back_pair[0, b] = part[:mid]
        back_pair[1, b] = part[mid:]
    back_pair_copy = remote(
        back_pair.at[1 - core],
        back_pair_in,
        pair_send_sem.at[n_block],
        pair_in_sem.at[n_block],
        partner,
    )

    for copy in (k_copy, v_copy, q_copy):
        copy.wait()
    kv_copies[0].wait_recv()
    kv_copies[1].wait_recv()
    for c in range(half, half + length, block):
        vt_ref[c : c + block, :] = v_ref[:, c : c + block].T

    def peers():
        for step in range(1, n_chip):
            yield lax.rem(chip + step, n_chip)

    def back_scatter():
        back_pair_copy.wait_recv()
        for b in range(n_block):
            total = back_pair[core, b] + back_pair_in[b]
            for p in range(n_chip):
                back_send[p, b] = piece(total, p).astype(sum_type)
        back_in[chip] = back_send[chip]
        for peer in peers():
            remote(
                back_send.at[peer],
                back_in.at[chip],
                rs_send_sem.at[n_block],
                rs_in_sem.at[n_block],
                {"head": peer * 2 + core},
            )

    def gather_send(buffer, index):
        for step in range(1, n_head):
            remote(
                buffer.at[me_h],
                buffer.at[me_h],
                ag_send_sem.at[index],
                ag_in_sem.at[index],
                {"head": lax.rem(me_h + step, n_head)},
            )

    def back_gather():
        settle(back_in.at[pl.ds(0, n_chip - 1)], rs_in_sem.at[n_block])
        total = back_in[0].astype(jnp.float32)
        for p in range(1, n_chip):
            total = total + back_in[p].astype(jnp.float32)
        back_all[me_h] = total.astype(jnp.bfloat16)
        gather_send(back_all, 2)

    def place(d):
        r = (d % 2) * mid + ((d // 2) // across) * pr
        c = ((d // 2) % across) * pc
        return r, c

    def back_finish():
        settle(back_all.at[pl.ds(0, n_head - 1)], ag_in_sem.at[2])
        for d in range(n_head):
            r, c = place(d)
            for b in range(n_block):
                back_ref[r : r + pr, b * block + c : b * block + c + pc] = back_all[d, b]

    def block_of(n):
        return lax.rem(n - 1 + sh * (n_block // 2), n_block)

    def act_product(n):
        rows = pl.ds(pl.multiple_of(block_of(n) * block, block), block)
        return lax.dot_general(
            down_ref[...], attn_ref[rows, :], NT, preferred_element_type=jnp.float32
        )

    def act_part(n):
        part = act_product(n)
        act_pair[n - 1, 0] = part[:mid]
        act_pair[n - 1, 1] = part[mid:]
        return remote(
            act_pair.at[n - 1, 1 - core],
            act_pair_in.at[n - 1],
            pair_send_sem.at[n - 1],
            pair_in_sem.at[n - 1],
            partner,
        )

    def act_scatter(n, copy):
        copy.wait_recv()
        total = act_pair[n - 1, core] + act_pair_in[n - 1]
        for p in range(n_chip):
            act_send[n - 1, p] = piece(total, p).astype(sum_type)
        act_in[n - 1, chip] = act_send[n - 1, chip]
        for peer in peers():
            remote(
                act_send.at[n - 1, peer],
                act_in.at[n - 1, chip],
                rs_send_sem.at[n - 1],
                rs_in_sem.at[n - 1],
                {"head": peer * 2 + core},
            )

    def last_scatter(n):
        part = act_product(n)
        for d in range(n_head):
            r, c = place(d)
            last_send[d] = part[r : r + pr, c : c + pc].astype(sum_type)
        last_in[me_h] = last_send[me_h]
        for step in range(1, n_head):
            peer = lax.rem(me_h + step, n_head)
            remote(
                last_send.at[peer],
                last_in.at[me_h],
                rs_send_sem.at[n - 1],
                rs_in_sem.at[n - 1],
                {"head": peer},
            )

    last_step = n_block - 1

    def act_gather(odd):
        for i, b in enumerate(range(odd, n_block, 2)):
            total = None
            for p in range(n_chip):
                n = b + 1 if p >= n_chip // 2 else (b + n_block // 2) % n_block + 1
                if n == last_step:
                    terms = [last_in[2 * p], last_in[2 * p + 1]]
                else:
                    terms = [act_in[n - 1, p]]
                for term in terms:
                    term = term.astype(jnp.float32)
                    total = term if total is None else total + term
            act_all[odd, me_h, i] = total.astype(jnp.bfloat16)
        gather_send(act_all.at[odd], odd)

    def act_finish(odd):
        settle(act_all.at[odd, pl.ds(0, n_head - 1)], ag_in_sem.at[odd])
        for d in range(n_head):
            r, c = place(d)
            for i, b in enumerate(range(odd, n_block, 2)):
                value = act_all[odd, d, i]
                low_ref[r : r + pr, b * block + c : b * block + c + pc] = value

    def up_part(odd):
        total = None
        for b in range(odd, n_block, 2):
            term = jnp.dot(
                low_ref[:, b * block : (b + 1) * block],
                grad_ref[b * block : (b + 1) * block, :],
                preferred_element_type=jnp.float32,
            )
            total = term if total is None else total + term
        return total

    sub = block // 2
    factor = math.log2(math.e) / math.sqrt(head_size)

    def attend(n, hooks):
        b = block_of(n)
        shifted_start = length if n <= n_block // 2 else 0
        start = pl.multiple_of(half + sh * (shifted_start - half), half)

        counts = (2 * n - 1, 2 * n)
        strips = (s0_ref, s1_ref)

        def rows_of(r):
            return pl.ds(pl.multiple_of(b * block + r * sub, sub), sub)

        def columns_of(h):
            return pl.ds(pl.multiple_of(h * head_size, head_size), head_size)

        def keys_of(j):
            return pl.ds(pl.multiple_of(start + j * sub, sub), sub)

        def score(r, h, j, top):
            value = jnp.dot(
                q_ref[rows_of(r), columns_of(h)],
                k_ref[:, keys_of(j)],
                preferred_element_type=jnp.float32,
            )
            if j == counts[r] - 1:
                row_index = lax.broadcasted_iota(jnp.int32, value.shape, 0)
                key_index = lax.broadcasted_iota(jnp.int32, value.shape, 1)
                value = jnp.where(key_index <= row_index, value, neg_big)
            strips[r][:, j * sub : (j + 1) * sub] = value
            for c in range(0, sub, 128):
                part = value[:, c : c + 128]
                top = part if top is None else jnp.maximum(top, part)
            return top

        def weigh(r, j, top, state):
            weights = jnp.exp2((strips[r][:, j * sub : (j + 1) * sub] - top) * factor)
            total, context = state
            for c in range(0, sub, 128):
                part = weights[:, c : c + 128]
                total = part if total is None else total + part
            term = jnp.dot(
                weights.astype(jnp.bfloat16),
                vt_ref[keys_of(j), :],
                preferred_element_type=jnp.float32,
            )
            return total, term if context is None else context + term

        def phase(r, h, top, next_r, next_h):
            top = jnp.max(top, axis=1, keepdims=True)
            state, next_top = (None, None), None
            for j in range(2 * n):
                if j < counts[next_r]:
                    next_top = score(next_r, next_h, j, next_top)
                if j < counts[r]:
                    state = weigh(r, j, top, state)
            total, context = state
            total = jnp.sum(total, axis=1, keepdims=True)
            attn_ref[rows_of(r), columns_of(h)] = (context * (1.0 / total)).astype(jnp.bfloat16)
            return next_top

        def body(h, top):
            for at, hook in hooks:
                pl.when(h == at)(hook)
            top = phase(0, h, top, 1, h)
            return phase(1, h, top, 0, jnp.minimum(h + 1, n_local - 1))

        first = None
        for j in range(counts[0]):
            first = score(0, 0, j, first)
        lax.fori_loop(0, n_local, body, first)

    pairs = {}
    attend(2, [(1, back_scatter)])
    pairs[2] = act_part(2)

    @pl.when(sh == 1)
    def _():
        for tail, forward in zip(tails, forwards):
            tail.wait_recv()
            forward.start()

    attend(1, [])
    pairs[1] = act_part(1)

    @pl.when(sh == 1)
    def _():
        for copy in forwards:
            copy.wait_recv()
        for c in range(0, half, block):
            vt_ref[c : c + block, :] = v_ref[:, c : c + block].T

    def early():
        act_scatter(2, pairs[2])
        act_scatter(1, pairs[1])
        back_gather()

    attend(4, [(1, early)])
    pairs[4] = act_part(4)

    def late():
        act_scatter(4, pairs[4])
        back_finish()

    def late_gather():
        for n in (2, 4):
            settle(act_in.at[n - 1, pl.ds(0, n_chip - 1)], rs_in_sem.at[n - 1])
        act_gather(1)

    attend(3, [(1, late), (3, late_gather)])
    last_scatter(3)

    def seq_scatter(kind, value):
        for p in range(n_seq):
            r, c = (p // s_across) * sr, (p % s_across) * sc
            seq_send[kind, p] = value[r : r + sr, c : c + sc]
        seq_in[kind, me_s] = seq_send[kind, me_s]
        for step in range(1, n_seq):
            peer = lax.rem(me_s + step, n_seq)
            remote(
                seq_send.at[kind, peer],
                seq_in.at[kind, me_s],
                seq_send_sem.at[kind, 0],
                seq_in_sem.at[kind, 0],
                {"seq": peer},
            )

    def seq_gather(kind):
        settle(seq_in.at[kind, pl.ds(0, n_seq - 1)], seq_in_sem.at[kind, 0])
        total = seq_in[kind, 0]
        for p in range(1, n_seq):
            total = total + seq_in[kind, p]
        seq_all[kind, me_s] = total * adapter_scale
        for step in range(1, n_seq):
            remote(
                seq_all.at[kind, me_s],
                seq_all.at[kind, me_s],
                seq_send_sem.at[kind, 1],
                seq_in_sem.at[kind, 1],
                {"seq": lax.rem(me_s + step, n_seq)},
            )

    act_finish(1)
    up_total = up_part(1)
    seq_scatter(
        0,
        jnp.dot(back_ref[...], attn_ref[...], preferred_element_type=jnp.float32),
    )
    settle(act_in.at[0, pl.ds(0, n_chip - 1)], rs_in_sem.at[0])
    settle(last_in.at[pl.ds(0, n_head - 1)], rs_in_sem.at[last_step - 1])
    act_gather(0)
    seq_gather(0)
    act_finish(0)
    seq_scatter(1, up_total + up_part(0))

    settle(seq_all.at[0, pl.ds(0, n_seq - 1)], seq_in_sem.at[0, 1])
    for p in range(n_seq):
        r, c = (p // s_across) * sr, (p % s_across) * sc
        down_out[r : r + sr, c : c + sc] = seq_all[0, p]
    seq_gather(1)
    settle(seq_all.at[1, pl.ds(0, n_seq - 1)], seq_in_sem.at[1, 1])
    for p in range(n_seq):
        r, c = (p // s_across) * sr, (p % s_across) * sc
        up_out[r : r + sr, c : c + sc] = seq_all[1, p]

    kv_copies[0].wait_send()
    kv_copies[1].wait_send()
    back_pair_copy.wait_send()
    settle(last_send.at[pl.ds(0, n_head - 1)], rs_send_sem.at[last_step - 1])
    for n in pairs:
        pairs[n].wait_send()
        settle(act_send.at[n - 1, pl.ds(0, n_chip - 1)], rs_send_sem.at[n - 1])
    settle(back_send.at[pl.ds(0, n_chip - 1)], rs_send_sem.at[n_block])
    settle(act_all.at[0, pl.ds(0, n_head - 1)], ag_send_sem.at[0])
    settle(act_all.at[1, pl.ds(0, n_head - 1)], ag_send_sem.at[1])
    settle(back_all.at[pl.ds(0, n_head - 1)], ag_send_sem.at[2])
    for kind in range(2):
        settle(seq_send.at[kind, pl.ds(0, n_seq - 1)], seq_send_sem.at[kind, 0])
        settle(seq_all.at[kind, pl.ds(0, n_seq - 1)], seq_send_sem.at[kind, 1])

    @pl.when(sh == 1)
    def _():
        for copy in tails + forwards:
            copy.wait_send()


def finish(low_ref, down_ref, up_ref, act_out, down_out, up_out):
    act_out[...] = low_ref[...].astype(jnp.float32)
    down_out[...] = down_ref[...]
    up_out[...] = up_ref[...]


def solution(mesh):
    n_seq, n_head = mesh.shape["seq"], mesh.shape["head"]
    n_chip = n_head // 2
    in_specs = (
        P("seq", "head"),
        P("head", "seq"),
        P("head", "seq"),
        P("head", None),
        P(None, "head"),
        P("seq", "head"),
    )
    out_specs = (P(None, "seq"), P("head", None), P(None, "head"))

    def on_device(queries, keys, values, down_factor, up_factor, gradient):
        length, width = queries.shape
        own = keys.shape[0]
        rank = up_factor.shape[0]
        n_block = length // block
        joined = length + length // 2
        pr, pc, _ = pieces_of(rank // 2, block, n_chip)
        sr, sc, _ = pieces_of(rank, block, n_seq)
        f32, b16 = jnp.float32, jnp.bfloat16
        dma = pltpu.SemaphoreType.DMA
        anywhere = pl.BlockSpec(memory_space=pl.ANY)
        vmem = pl.BlockSpec(memory_space=pltpu.VMEM)
        low, down, up = pl.pallas_call(
            functools.partial(kernel, n_seq, n_head),
            out_shape=(
                jax.ShapeDtypeStruct((rank, length), b16),
                jax.ShapeDtypeStruct((rank, width), f32),
                jax.ShapeDtypeStruct((rank, width), f32),
            ),
            in_specs=[anywhere, anywhere, anywhere, vmem, vmem, anywhere],
            out_specs=(vmem, vmem, vmem),
            scratch_shapes=[
                pltpu.VMEM((length, width), b16),
                pltpu.VMEM((length, width), b16),
                pltpu.VMEM((2 * own, joined), b16),
                pltpu.VMEM((2 * own, joined), b16),
                pltpu.VMEM((joined, 2 * own), b16),
                pltpu.VMEM((length, width), b16),
                pltpu.VMEM((2, n_block, rank // 2, block), f32),
                pltpu.VMEM((n_block, rank // 2, block), f32),
                pltpu.VMEM((n_chip, n_block, pr, pc), sum_type),
                pltpu.VMEM((n_chip, n_block, pr, pc), sum_type),
                pltpu.VMEM((n_head, n_block, pr, pc), b16),
                pltpu.VMEM((rank, length), b16),
                pltpu.VMEM((n_block, 2, rank // 2, block), f32),
                pltpu.VMEM((n_block, rank // 2, block), f32),
                pltpu.VMEM((n_block, n_chip, pr, pc), sum_type),
                pltpu.VMEM((n_block, n_chip, pr, pc), sum_type),
                pltpu.VMEM((2, n_head, n_block // 2, pr, pc), b16),
                pltpu.VMEM((n_head, pr, pc), sum_type),
                pltpu.VMEM((n_head, pr, pc), sum_type),
                pltpu.VMEM((block // 2, length), f32),
                pltpu.VMEM((block // 2, length), f32),
                pltpu.VMEM((2, n_seq, sr, sc), f32),
                pltpu.VMEM((2, n_seq, sr, sc), f32),
                pltpu.VMEM((2, n_seq, sr, sc), f32),
                dma((4,)),
                dma((6,)),
                dma((6,)),
                dma((n_block + 1,)),
                dma((n_block + 1,)),
                dma((n_block + 1,)),
                dma((n_block + 1,)),
                dma((3,)),
                dma((3,)),
                dma((2, 2)),
                dma((2, 2)),
            ],
            compiler_params=pltpu.CompilerParams(
                collective_id=0, has_side_effects=True, vmem_limit_bytes=56 * 2**20
            ),
            cost_estimate=pl.CostEstimate(
                flops=6 * 10**9, bytes_accessed=8 * 2**20, transcendentals=10**7
            ),
        )(queries, keys, values, down_factor.T, up_factor, gradient)
        activations, down, up = pl.pallas_call(
            finish,
            out_shape=(
                jax.ShapeDtypeStruct((rank, length), f32),
                jax.ShapeDtypeStruct((rank, width), f32),
                jax.ShapeDtypeStruct((rank, width), f32),
            ),
            in_specs=[vmem, vmem, vmem],
            out_specs=(vmem, vmem, vmem),
        )(low, down, up)
        return activations, down.T, up

    return jax.shard_map(
        on_device, mesh=mesh, in_specs=in_specs, out_specs=out_specs, check_vma=False
    )
```

```python
import functools
import math

import jax
import jax.numpy as jnp
from jax import lax
from jax.experimental import pallas as pl
from jax.experimental.pallas import tpu as pltpu
from jax.sharding import PartitionSpec as P

neg_big = -1e30
adapter_scale = 2.0
head_size = 128
block = 512
sum_type = jnp.bfloat16


def pieces_of(rows, columns, count):
    across = min(count, columns // 128)
    down = count // across
    return rows // down, columns // across, across


def kernel(
    n_seq,
    n_head,
    q_hbm,
    k_hbm,
    v_hbm,
    down_ref,
    up_ref,
    grad_hbm,
    low_ref,
    down_out,
    up_out,
    q_ref,
    grad_ref,
    k_ref,
    v_ref,
    vt_ref,
    attn_ref,
    back_pair,
    back_pair_in,
    back_send,
    back_in,
    back_all,
    back_ref,
    act_pair,
    act_pair_in,
    act_send,
    act_in,
    act_all,
    last_send,
    last_in,
    s0_ref,
    s1_ref,
    down_t,
    up_send,
    up_all,
    seq_send,
    seq_in,
    seq_all,
    local_sem,
    kv_send,
    kv_in,
    pair_send_sem,
    pair_in_sem,
    rs_send_sem,
    rs_in_sem,
    ag_send_sem,
    ag_in_sem,
    seq_send_sem,
    seq_in_sem,
):
    me_s, me_h = lax.axis_index("seq"), lax.axis_index("head")
    n_chip = n_head // 2
    chip, core = me_h // 2, me_h % 2
    partner = {"head": me_h + 1 - 2 * core}
    sh = 1 - me_h // (n_head // 2)
    length = q_ref.shape[0]
    half = length // 2
    n_local = q_ref.shape[1] // head_size
    rank = up_ref.shape[0]
    mid = rank // 2
    own = k_hbm.shape[0]
    n_block = length // block
    pr, pc, across = pieces_of(mid, block, n_chip)
    sr, sc, s_across = pieces_of(rank, block, n_seq)

    def piece(value, index):
        r, c = (index // across) * pr, (index % across) * pc
        return value[r : r + pr, c : c + pc]

    def remote(src, dst, send, recv, device):
        copy = pltpu.make_async_remote_copy(
            src_ref=src,
            dst_ref=dst,
            send_sem=send,
            recv_sem=recv,
            device_id=device,
            device_id_type=pl.DeviceIdType.MESH,
        )
        copy.start()
        return copy

    def settle(ref, sem):
        pltpu.make_async_copy(ref, ref, sem).wait()

    barrier = pltpu.get_barrier_semaphore()
    for step in range(1, n_head):
        pl.semaphore_signal(
            barrier,
            inc=1,
            device_id={"head": lax.rem(me_h + step, n_head)},
            device_id_type=pl.DeviceIdType.MESH,
        )
    for step in range(1, n_seq):
        pl.semaphore_signal(
            barrier,
            inc=1,
            device_id={"seq": lax.rem(me_s + step, n_seq)},
            device_id_type=pl.DeviceIdType.MESH,
        )

    own_rows = pl.ds(pl.multiple_of(core * own, own), own)
    grad_copy = pltpu.make_async_copy(grad_hbm, grad_ref, local_sem.at[0])
    k_copy = pltpu.make_async_copy(k_hbm, k_ref.at[own_rows, pl.ds(half, length)], local_sem.at[1])
    v_copy = pltpu.make_async_copy(v_hbm, v_ref.at[own_rows, pl.ds(half, length)], local_sem.at[2])
    q_copy = pltpu.make_async_copy(q_hbm, q_ref, local_sem.at[3])
    for copy in (grad_copy, k_copy, v_copy, q_copy):
        copy.start()

    pl.semaphore_wait(barrier, n_head + n_seq - 2)

    kv_copies = []
    for i, (src, dst) in enumerate(((k_hbm, k_ref), (v_hbm, v_ref))):
        kv_copies.append(
            remote(
                src,
                dst.at[own_rows, pl.ds(half, length)],
                kv_send.at[i],
                kv_in.at[i],
                partner,
            )
        )

    def tail_copy(i, src, dst):
        return pltpu.make_async_remote_copy(
            src_ref=src.at[:, pl.ds(half, half)],
            dst_ref=dst.at[own_rows, pl.ds(0, half)],
            send_sem=kv_send.at[2 + i],
            recv_sem=kv_in.at[2 + i],
            device_id={"seq": lax.rem(me_s + 1, n_seq)},
            device_id_type=pl.DeviceIdType.MESH,
        )

    def forward_copy(i, ref):
        return pltpu.make_async_remote_copy(
            src_ref=ref.at[own_rows, pl.ds(0, half)],
            dst_ref=ref.at[own_rows, pl.ds(0, half)],
            send_sem=kv_send.at[4 + i],
            recv_sem=kv_in.at[4 + i],
            device_id=partner,
            device_id_type=pl.DeviceIdType.MESH,
        )

    tails = [tail_copy(0, k_hbm, k_ref), tail_copy(1, v_hbm, v_ref)]
    forwards = [forward_copy(0, k_ref), forward_copy(1, v_ref)]

    @pl.when(sh == 1)
    def _():
        for copy in tails:
            copy.start()

    up_t = up_ref[...].T
    grad_copy.wait()
    for b in range(n_block):
        part = jnp.dot(
            grad_ref[b * block : (b + 1) * block, :], up_t, preferred_element_type=jnp.float32
        ).T
        back_pair[0, b] = part[:mid]
        back_pair[1, b] = part[mid:]
    back_pair_copy = remote(
        back_pair.at[1 - core],
        back_pair_in,
        pair_send_sem.at[n_block],
        pair_in_sem.at[n_block],
        partner,
    )

    down_t[...] = down_ref[...].T
    for copy in (k_copy, v_copy, q_copy):
        copy.wait()
    kv_copies[0].wait_recv()
    kv_copies[1].wait_recv()
    for c in range(half, half + length, block):
        vt_ref[c : c + block, :] = v_ref[:, c : c + block].T

    def peers():
        for step in range(1, n_chip):
            yield lax.rem(chip + step, n_chip)

    def back_scatter():
        back_pair_copy.wait_recv()
        for b in range(n_block):
            total = back_pair[core, b] + back_pair_in[b]
            for p in range(n_chip):
                back_send[p, b] = piece(total, p).astype(sum_type)
        back_in[chip] = back_send[chip]
        for peer in peers():
            remote(
                back_send.at[peer],
                back_in.at[chip],
                rs_send_sem.at[n_block],
                rs_in_sem.at[n_block],
                {"head": peer * 2 + core},
            )

    def gather_send(buffer, index):
        for step in range(1, n_head):
            remote(
                buffer.at[me_h],
                buffer.at[me_h],
                ag_send_sem.at[index],
                ag_in_sem.at[index],
                {"head": lax.rem(me_h + step, n_head)},
            )

    def back_gather():
        settle(back_in.at[pl.ds(0, n_chip - 1)], rs_in_sem.at[n_block])
        total = back_in[0].astype(jnp.float32)
        for p in range(1, n_chip):
            total = total + back_in[p].astype(jnp.float32)
        back_all[me_h] = total.astype(jnp.bfloat16)
        gather_send(back_all, 2)

    def place(d):
        r = (d % 2) * mid + ((d // 2) // across) * pr
        c = ((d // 2) % across) * pc
        return r, c

    def back_finish():
        settle(back_all.at[pl.ds(0, n_head - 1)], ag_in_sem.at[2])
        for d in range(n_head):
            r, c = place(d)
            for b in range(n_block):
                back_ref[r : r + pr, b * block + c : b * block + c + pc] = back_all[d, b]

    def block_of(n):
        return lax.rem(n - 1 + sh * (n_block // 2), n_block)

    def act_product(n):
        rows = pl.ds(pl.multiple_of(block_of(n) * block, block), block)
        return jnp.dot(attn_ref[rows, :], down_t[...], preferred_element_type=jnp.float32).T

    def act_part(n):
        part = act_product(n)
        act_pair[n - 1, 0] = part[:mid]
        act_pair[n - 1, 1] = part[mid:]
        return remote(
            act_pair.at[n - 1, 1 - core],
            act_pair_in.at[n - 1],
            pair_send_sem.at[n - 1],
            pair_in_sem.at[n - 1],
            partner,
        )

    def act_scatter(n, copy):
        copy.wait_recv()
        total = act_pair[n - 1, core] + act_pair_in[n - 1]
        for p in range(n_chip):
            act_send[n - 1, p] = piece(total, p).astype(sum_type)
        act_in[n - 1, chip] = act_send[n - 1, chip]
        for peer in peers():
            remote(
                act_send.at[n - 1, peer],
                act_in.at[n - 1, chip],
                rs_send_sem.at[n - 1],
                rs_in_sem.at[n - 1],
                {"head": peer * 2 + core},
            )

    def last_scatter(n):
        part = act_product(n)
        for d in range(n_head):
            r, c = place(d)
            last_send[d] = part[r : r + pr, c : c + pc].astype(sum_type)
        last_in[me_h] = last_send[me_h]
        for step in range(1, n_head):
            peer = lax.rem(me_h + step, n_head)
            remote(
                last_send.at[peer],
                last_in.at[me_h],
                rs_send_sem.at[n - 1],
                rs_in_sem.at[n - 1],
                {"head": peer},
            )

    last_step = n_block - 1

    def act_gather(odd):
        for i, b in enumerate(range(odd, n_block, 2)):
            total = None
            for p in range(n_chip):
                n = b + 1 if p >= n_chip // 2 else (b + n_block // 2) % n_block + 1
                if n == last_step:
                    terms = [last_in[2 * p], last_in[2 * p + 1]]
                else:
                    terms = [act_in[n - 1, p]]
                for term in terms:
                    term = term.astype(jnp.float32)
                    total = term if total is None else total + term
            act_all[odd, me_h, i] = total.astype(jnp.bfloat16)
        gather_send(act_all.at[odd], odd)

    def act_finish(odd):
        settle(act_all.at[odd, pl.ds(0, n_head - 1)], ag_in_sem.at[odd])
        for d in range(n_head):
            r, c = place(d)
            for i, b in enumerate(range(odd, n_block, 2)):
                value = act_all[odd, d, i]
                low_ref[r : r + pr, b * block + c : b * block + c + pc] = value

    def up_part(odd):
        total = None
        for b in range(odd, n_block, 2):
            term = jnp.dot(
                low_ref[:, b * block : (b + 1) * block],
                grad_ref[b * block : (b + 1) * block, :],
                preferred_element_type=jnp.float32,
            )
            total = term if total is None else total + term
        return total

    sub = block // 2
    factor = math.log2(math.e) / math.sqrt(head_size)

    def attend(n, hooks):
        b = block_of(n)
        shifted_start = length if n <= n_block // 2 else 0
        start = pl.multiple_of(half + sh * (shifted_start - half), half)

        counts = (2 * n - 1, 2 * n)
        strips = (s0_ref, s1_ref)

        def rows_of(r):
            return pl.ds(pl.multiple_of(b * block + r * sub, sub), sub)

        def columns_of(h):
            return pl.ds(pl.multiple_of(h * head_size, head_size), head_size)

        def keys_of(j, wide=1):
            return pl.ds(pl.multiple_of(start + j * sub, sub), wide * sub)

        def score(r, h, j, top):
            value = jnp.dot(
                q_ref[rows_of(r), columns_of(h)],
                k_ref[:, keys_of(j)],
                preferred_element_type=jnp.float32,
            )
            if j == counts[r] - 1:
                row_index = lax.broadcasted_iota(jnp.int32, value.shape, 0)
                key_index = lax.broadcasted_iota(jnp.int32, value.shape, 1)
                value = jnp.where(key_index <= row_index, value, neg_big)
            strips[r][:, j * sub : (j + 1) * sub] = value
            for c in range(0, sub, 128):
                part = value[:, c : c + 128]
                top = part if top is None else jnp.maximum(top, part)
            return top

        def weigh(r, j, wide, top, state):
            weights = jnp.exp2((strips[r][:, j * sub : (j + wide) * sub] - top) * factor)
            total, context = state
            for c in range(0, wide * sub, 128):
                part = weights[:, c : c + 128]
                total = part if total is None else total + part
            term = jnp.dot(
                weights.astype(jnp.bfloat16),
                vt_ref[keys_of(j, wide), :],
                preferred_element_type=jnp.float32,
            )
            return total, term if context is None else context + term

        def phase(r, h, top, next_r, next_h):
            top = jnp.max(top, axis=1, keepdims=True)
            state, next_top = (None, None), None
            for j in range(2 * n):
                if j < counts[next_r]:
                    next_top = score(next_r, next_h, j, next_top)
                if j % 2 == 0 and j < counts[r]:
                    state = weigh(r, j, min(2, counts[r] - j), top, state)
            total, context = state
            total = jnp.sum(total, axis=1, keepdims=True)
            attn_ref[rows_of(r), columns_of(h)] = (context * (1.0 / total)).astype(jnp.bfloat16)
            return next_top

        def body(h, top):
            for at, hook in hooks:
                pl.when(h == at)(hook)
            top = phase(0, h, top, 1, h)
            return phase(1, h, top, 0, jnp.minimum(h + 1, n_local - 1))

        first = None
        for j in range(counts[0]):
            first = score(0, 0, j, first)
        lax.fori_loop(0, n_local, body, first)

    pairs = {}
    attend(2, [(1, back_scatter)])
    pairs[2] = act_part(2)

    @pl.when(sh == 1)
    def _():
        for tail, forward in zip(tails, forwards):
            tail.wait_recv()
            forward.start()

    attend(1, [])
    pairs[1] = act_part(1)

    @pl.when(sh == 1)
    def _():
        for copy in forwards:
            copy.wait_recv()
        for c in range(0, half, block):
            vt_ref[c : c + block, :] = v_ref[:, c : c + block].T

    def early():
        act_scatter(2, pairs[2])
        act_scatter(1, pairs[1])
        back_gather()

    attend(4, [(1, early)])
    pairs[4] = act_part(4)

    def late():
        act_scatter(4, pairs[4])
        back_finish()

    def late_gather():
        for n in (2, 4):
            settle(act_in.at[n - 1, pl.ds(0, n_chip - 1)], rs_in_sem.at[n - 1])
        act_gather(1)

    attend(3, [(1, late), (3, late_gather)])
    last_scatter(3)

    def seq_scatter(value):
        for p in range(n_seq):
            r, c = (p // s_across) * sr, (p % s_across) * sc
            seq_send[p] = value[r : r + sr, c : c + sc]
        seq_in[me_s] = seq_send[me_s]
        for step in range(1, n_seq):
            peer = lax.rem(me_s + step, n_seq)
            remote(
                seq_send.at[peer],
                seq_in.at[me_s],
                seq_send_sem.at[0, 0],
                seq_in_sem.at[0, 0],
                {"seq": peer},
            )

    def seq_gather():
        settle(seq_in.at[pl.ds(0, n_seq - 1)], seq_in_sem.at[0, 0])
        total = seq_in[0]
        for p in range(1, n_seq):
            total = total + seq_in[p]
        seq_all[me_s] = total * adapter_scale
        for step in range(1, n_seq):
            remote(
                seq_all.at[me_s],
                seq_all.at[me_s],
                seq_send_sem.at[0, 1],
                seq_in_sem.at[0, 1],
                {"seq": lax.rem(me_s + step, n_seq)},
            )

    act_finish(1)
    up_total = up_part(1)
    seq_scatter(jnp.dot(back_ref[...], attn_ref[...], preferred_element_type=jnp.float32))
    settle(act_in.at[0, pl.ds(0, n_chip - 1)], rs_in_sem.at[0])
    settle(last_in.at[pl.ds(0, n_head - 1)], rs_in_sem.at[last_step - 1])
    act_gather(0)
    seq_gather()
    act_finish(0)
    up_send[...] = (up_total + up_part(0)).astype(sum_type)
    for step in range(1, n_seq):
        remote(
            up_send,
            up_all.at[me_s],
            seq_send_sem.at[1, 0],
            seq_in_sem.at[1, 0],
            {"seq": lax.rem(me_s + step, n_seq)},
        )
    up_all[me_s] = up_send[...]

    settle(seq_all.at[pl.ds(0, n_seq - 1)], seq_in_sem.at[0, 1])
    for p in range(n_seq):
        r, c = (p // s_across) * sr, (p % s_across) * sc
        down_out[r : r + sr, c : c + sc] = seq_all[p]
    settle(up_all.at[pl.ds(0, n_seq - 1)], seq_in_sem.at[1, 0])
    total = up_all[0].astype(jnp.float32)
    for p in range(1, n_seq):
        total = total + up_all[p].astype(jnp.float32)
    up_out[...] = total * adapter_scale

    kv_copies[0].wait_send()
    kv_copies[1].wait_send()
    back_pair_copy.wait_send()
    settle(last_send.at[pl.ds(0, n_head - 1)], rs_send_sem.at[last_step - 1])
    for n in pairs:
        pairs[n].wait_send()
        settle(act_send.at[n - 1, pl.ds(0, n_chip - 1)], rs_send_sem.at[n - 1])
    settle(back_send.at[pl.ds(0, n_chip - 1)], rs_send_sem.at[n_block])
    settle(act_all.at[0, pl.ds(0, n_head - 1)], ag_send_sem.at[0])
    settle(act_all.at[1, pl.ds(0, n_head - 1)], ag_send_sem.at[1])
    settle(back_all.at[pl.ds(0, n_head - 1)], ag_send_sem.at[2])
    settle(seq_send.at[pl.ds(0, n_seq - 1)], seq_send_sem.at[0, 0])
    settle(seq_all.at[pl.ds(0, n_seq - 1)], seq_send_sem.at[0, 1])
    settle(up_all.at[pl.ds(0, n_seq - 1)], seq_send_sem.at[1, 0])

    @pl.when(sh == 1)
    def _():
        for copy in tails + forwards:
            copy.wait_send()


def finish(low_ref, down_ref, up_ref, act_out, down_out, up_out):
    act_out[...] = low_ref[...].astype(jnp.float32)
    down_out[...] = down_ref[...]
    up_out[...] = up_ref[...]


def solution(mesh):
    n_seq, n_head = mesh.shape["seq"], mesh.shape["head"]
    n_chip = n_head // 2
    in_specs = (
        P("seq", "head"),
        P("head", "seq"),
        P("head", "seq"),
        P("head", None),
        P(None, "head"),
        P("seq", "head"),
    )
    out_specs = (P(None, "seq"), P("head", None), P(None, "head"))

    def on_device(queries, keys, values, down_factor, up_factor, gradient):
        length, width = queries.shape
        own = keys.shape[0]
        rank = up_factor.shape[0]
        n_block = length // block
        joined = length + length // 2
        pr, pc, _ = pieces_of(rank // 2, block, n_chip)
        sr, sc, _ = pieces_of(rank, block, n_seq)
        f32, b16 = jnp.float32, jnp.bfloat16
        dma = pltpu.SemaphoreType.DMA
        anywhere = pl.BlockSpec(memory_space=pl.ANY)
        vmem = pl.BlockSpec(memory_space=pltpu.VMEM)
        low, down, up = pl.pallas_call(
            functools.partial(kernel, n_seq, n_head),
            out_shape=(
                jax.ShapeDtypeStruct((rank, length), b16),
                jax.ShapeDtypeStruct((rank, width), f32),
                jax.ShapeDtypeStruct((rank, width), f32),
            ),
            in_specs=[anywhere, anywhere, anywhere, vmem, vmem, anywhere],
            out_specs=(vmem, vmem, vmem),
            scratch_shapes=[
                pltpu.VMEM((length, width), b16),
                pltpu.VMEM((length, width), b16),
                pltpu.VMEM((2 * own, joined), b16),
                pltpu.VMEM((2 * own, joined), b16),
                pltpu.VMEM((joined, 2 * own), b16),
                pltpu.VMEM((length, width), b16),
                pltpu.VMEM((2, n_block, rank // 2, block), f32),
                pltpu.VMEM((n_block, rank // 2, block), f32),
                pltpu.VMEM((n_chip, n_block, pr, pc), sum_type),
                pltpu.VMEM((n_chip, n_block, pr, pc), sum_type),
                pltpu.VMEM((n_head, n_block, pr, pc), b16),
                pltpu.VMEM((rank, length), b16),
                pltpu.VMEM((n_block, 2, rank // 2, block), f32),
                pltpu.VMEM((n_block, rank // 2, block), f32),
                pltpu.VMEM((n_block, n_chip, pr, pc), sum_type),
                pltpu.VMEM((n_block, n_chip, pr, pc), sum_type),
                pltpu.VMEM((2, n_head, n_block // 2, pr, pc), b16),
                pltpu.VMEM((n_head, pr, pc), sum_type),
                pltpu.VMEM((n_head, pr, pc), sum_type),
                pltpu.VMEM((block // 2, length), f32),
                pltpu.VMEM((block // 2, length), f32),
                pltpu.VMEM((width, rank), b16),
                pltpu.VMEM((rank, width), sum_type),
                pltpu.VMEM((n_seq, rank, width), sum_type),
                pltpu.VMEM((n_seq, sr, sc), f32),
                pltpu.VMEM((n_seq, sr, sc), f32),
                pltpu.VMEM((n_seq, sr, sc), f32),
                dma((4,)),
                dma((6,)),
                dma((6,)),
                dma((n_block + 1,)),
                dma((n_block + 1,)),
                dma((n_block + 1,)),
                dma((n_block + 1,)),
                dma((3,)),
                dma((3,)),
                dma((2, 2)),
                dma((2, 2)),
            ],
            compiler_params=pltpu.CompilerParams(
                collective_id=0, has_side_effects=True, vmem_limit_bytes=56 * 2**20
            ),
            cost_estimate=pl.CostEstimate(
                flops=6 * 10**9, bytes_accessed=8 * 2**20, transcendentals=10**7
            ),
        )(queries, keys, values, down_factor.T, up_factor, gradient)
        activations, down, up = pl.pallas_call(
            finish,
            out_shape=(
                jax.ShapeDtypeStruct((rank, length), f32),
                jax.ShapeDtypeStruct((rank, width), f32),
                jax.ShapeDtypeStruct((rank, width), f32),
            ),
            in_specs=[vmem, vmem, vmem],
            out_specs=(vmem, vmem, vmem),
        )(low, down, up)
        return activations, down.T, up

    return jax.shard_map(
        on_device, mesh=mesh, in_specs=in_specs, out_specs=out_specs, check_vma=False
    )
```

```python
import functools
import math

import jax
import jax.numpy as jnp
from jax import lax
from jax.experimental import pallas as pl
from jax.experimental.pallas import tpu as pltpu
from jax.sharding import PartitionSpec as P

neg_big = -1e30
adapter_scale = 2.0
head_size = 128
block = 512
sum_type = jnp.bfloat16


def pieces_of(rows, columns, count):
    across = min(count, columns // 128)
    down = count // across
    return rows // down, columns // across, across


def kernel(
    n_seq,
    n_head,
    q_hbm,
    k_hbm,
    v_hbm,
    down_ref,
    up_ref,
    grad_hbm,
    low_hbm,
    down_hbm,
    up_out,
    low_ref,
    down_out,
    q_ref,
    grad_ref,
    k_ref,
    v_ref,
    vt_ref,
    attn_ref,
    back_pair,
    back_pair_in,
    back_send,
    back_in,
    back_all,
    back_ref,
    act_pair,
    act_pair_in,
    act_send,
    act_in,
    act_all,
    last_send,
    last_in,
    s0_ref,
    s1_ref,
    down_t,
    up_send,
    up_all,
    seq_send,
    seq_in,
    seq_all,
    local_sem,
    kv_send,
    kv_in,
    pair_send_sem,
    pair_in_sem,
    rs_send_sem,
    rs_in_sem,
    ag_send_sem,
    ag_in_sem,
    seq_send_sem,
    seq_in_sem,
):
    me_s, me_h = lax.axis_index("seq"), lax.axis_index("head")
    n_chip = n_head // 2
    chip, core = me_h // 2, me_h % 2
    partner = {"head": me_h + 1 - 2 * core}
    sh = 1 - me_h // (n_head // 2)
    length = q_ref.shape[0]
    half = length // 2
    n_local = q_ref.shape[1] // head_size
    rank = up_ref.shape[0]
    mid = rank // 2
    own = k_hbm.shape[0]
    n_block = length // block
    pr, pc, across = pieces_of(mid, block, n_chip)
    sr, sc, s_across = pieces_of(rank, block, n_seq)

    def piece(value, index):
        r, c = (index // across) * pr, (index % across) * pc
        return value[r : r + pr, c : c + pc]

    def remote(src, dst, send, recv, device):
        copy = pltpu.make_async_remote_copy(
            src_ref=src,
            dst_ref=dst,
            send_sem=send,
            recv_sem=recv,
            device_id=device,
            device_id_type=pl.DeviceIdType.MESH,
        )
        copy.start()
        return copy

    def settle(ref, sem):
        pltpu.make_async_copy(ref, ref, sem).wait()

    barrier = pltpu.get_barrier_semaphore()
    for step in range(1, n_head):
        pl.semaphore_signal(
            barrier,
            inc=1,
            device_id={"head": lax.rem(me_h + step, n_head)},
            device_id_type=pl.DeviceIdType.MESH,
        )
    for step in range(1, n_seq):
        pl.semaphore_signal(
            barrier,
            inc=1,
            device_id={"seq": lax.rem(me_s + step, n_seq)},
            device_id_type=pl.DeviceIdType.MESH,
        )

    own_rows = pl.ds(pl.multiple_of(core * own, own), own)
    grad_copy = pltpu.make_async_copy(grad_hbm, grad_ref, local_sem.at[0])
    k_copy = pltpu.make_async_copy(k_hbm, k_ref.at[own_rows, pl.ds(half, length)], local_sem.at[1])
    v_copy = pltpu.make_async_copy(v_hbm, v_ref.at[own_rows, pl.ds(half, length)], local_sem.at[2])
    q_copy = pltpu.make_async_copy(q_hbm, q_ref, local_sem.at[3])
    for copy in (grad_copy, k_copy, v_copy, q_copy):
        copy.start()

    pl.semaphore_wait(barrier, n_head + n_seq - 2)

    kv_copies = []
    for i, (src, dst) in enumerate(((k_hbm, k_ref), (v_hbm, v_ref))):
        kv_copies.append(
            remote(
                src,
                dst.at[own_rows, pl.ds(half, length)],
                kv_send.at[i],
                kv_in.at[i],
                partner,
            )
        )

    def tail_copy(i, src, dst):
        return pltpu.make_async_remote_copy(
            src_ref=src.at[:, pl.ds(half, half)],
            dst_ref=dst.at[own_rows, pl.ds(0, half)],
            send_sem=kv_send.at[2 + i],
            recv_sem=kv_in.at[2 + i],
            device_id={"seq": lax.rem(me_s + 1, n_seq)},
            device_id_type=pl.DeviceIdType.MESH,
        )

    def forward_copy(i, ref):
        return pltpu.make_async_remote_copy(
            src_ref=ref.at[own_rows, pl.ds(0, half)],
            dst_ref=ref.at[own_rows, pl.ds(0, half)],
            send_sem=kv_send.at[4 + i],
            recv_sem=kv_in.at[4 + i],
            device_id=partner,
            device_id_type=pl.DeviceIdType.MESH,
        )

    tails = [tail_copy(0, k_hbm, k_ref), tail_copy(1, v_hbm, v_ref)]
    forwards = [forward_copy(0, k_ref), forward_copy(1, v_ref)]

    @pl.when(sh == 1)
    def _():
        for copy in tails:
            copy.start()

    up_t = up_ref[...].T
    grad_copy.wait()
    for b in range(n_block):
        part = jnp.dot(
            grad_ref[b * block : (b + 1) * block, :], up_t, preferred_element_type=jnp.float32
        ).T
        back_pair[0, b] = part[:mid]
        back_pair[1, b] = part[mid:]
    back_pair_copy = remote(
        back_pair.at[1 - core],
        back_pair_in,
        pair_send_sem.at[n_block],
        pair_in_sem.at[n_block],
        partner,
    )

    down_t[...] = down_ref[...].T
    vt_ref[:, head_size:] = jnp.ones((vt_ref.shape[0], head_size), jnp.bfloat16)
    for copy in (k_copy, v_copy, q_copy):
        copy.wait()
    kv_copies[0].wait_recv()
    kv_copies[1].wait_recv()
    for c in range(half, half + length, block):
        vt_ref[c : c + block, :head_size] = v_ref[:, c : c + block].T

    def peers():
        for step in range(1, n_chip):
            yield lax.rem(chip + step, n_chip)

    def back_scatter():
        back_pair_copy.wait_recv()
        for b in range(n_block):
            total = back_pair[core, b] + back_pair_in[b]
            for p in range(n_chip):
                back_send[p, b] = piece(total, p).astype(sum_type)
        back_in[chip] = back_send[chip]
        for peer in peers():
            remote(
                back_send.at[peer],
                back_in.at[chip],
                rs_send_sem.at[n_block],
                rs_in_sem.at[n_block],
                {"head": peer * 2 + core},
            )

    def gather_send(buffer, index):
        for step in range(1, n_head):
            remote(
                buffer.at[me_h],
                buffer.at[me_h],
                ag_send_sem.at[index],
                ag_in_sem.at[index],
                {"head": lax.rem(me_h + step, n_head)},
            )

    def back_gather():
        settle(back_in.at[pl.ds(0, n_chip - 1)], rs_in_sem.at[n_block])
        total = back_in[0].astype(jnp.float32)
        for p in range(1, n_chip):
            total = total + back_in[p].astype(jnp.float32)
        back_all[me_h] = total.astype(jnp.bfloat16)
        gather_send(back_all, 2)

    def place(d):
        r = (d % 2) * mid + ((d // 2) // across) * pr
        c = ((d // 2) % across) * pc
        return r, c

    def back_finish():
        settle(back_all.at[pl.ds(0, n_head - 1)], ag_in_sem.at[2])
        for d in range(n_head):
            r, c = place(d)
            for b in range(n_block):
                back_ref[r : r + pr, b * block + c : b * block + c + pc] = back_all[d, b]

    def block_of(n):
        return lax.rem(n - 1 + sh * (n_block // 2), n_block)

    def act_product(n):
        rows = pl.ds(pl.multiple_of(block_of(n) * block, block), block)
        return jnp.dot(attn_ref[rows, :], down_t[...], preferred_element_type=jnp.float32).T

    def act_part(n):
        part = act_product(n)
        act_pair[n - 1, 0] = part[:mid]
        act_pair[n - 1, 1] = part[mid:]
        return remote(
            act_pair.at[n - 1, 1 - core],
            act_pair_in.at[n - 1],
            pair_send_sem.at[n - 1],
            pair_in_sem.at[n - 1],
            partner,
        )

    def act_scatter(n, copy):
        copy.wait_recv()
        total = act_pair[n - 1, core] + act_pair_in[n - 1]
        for p in range(n_chip):
            act_send[n - 1, p] = piece(total, p).astype(sum_type)
        act_in[n - 1, chip] = act_send[n - 1, chip]
        for peer in peers():
            remote(
                act_send.at[n - 1, peer],
                act_in.at[n - 1, chip],
                rs_send_sem.at[n - 1],
                rs_in_sem.at[n - 1],
                {"head": peer * 2 + core},
            )

    def last_scatter(n):
        part = act_product(n)
        for d in range(n_head):
            r, c = place(d)
            last_send[d] = part[r : r + pr, c : c + pc].astype(sum_type)
        last_in[me_h] = last_send[me_h]
        for step in range(1, n_head):
            peer = lax.rem(me_h + step, n_head)
            remote(
                last_send.at[peer],
                last_in.at[me_h],
                rs_send_sem.at[n - 1],
                rs_in_sem.at[n - 1],
                {"head": peer},
            )

    last_step = n_block - 1

    def act_gather(odd):
        for i, b in enumerate(range(odd, n_block, 2)):
            total = None
            for p in range(n_chip):
                n = b + 1 if p >= n_chip // 2 else (b + n_block // 2) % n_block + 1
                if n == last_step:
                    terms = [last_in[2 * p], last_in[2 * p + 1]]
                else:
                    terms = [act_in[n - 1, p]]
                for term in terms:
                    term = term.astype(jnp.float32)
                    total = term if total is None else total + term
            act_all[odd, me_h, i] = total.astype(jnp.bfloat16)
        gather_send(act_all.at[odd], odd)

    def act_finish(odd):
        settle(act_all.at[odd, pl.ds(0, n_head - 1)], ag_in_sem.at[odd])
        for d in range(n_head):
            r, c = place(d)
            for i, b in enumerate(range(odd, n_block, 2)):
                value = act_all[odd, d, i]
                low_ref[r : r + pr, b * block + c : b * block + c + pc] = value

    def up_part(odd):
        total = None
        for b in range(odd, n_block, 2):
            term = jnp.dot(
                low_ref[:, b * block : (b + 1) * block],
                grad_ref[b * block : (b + 1) * block, :],
                preferred_element_type=jnp.float32,
            )
            total = term if total is None else total + term
        return total

    sub = block // 2
    factor = math.log2(math.e) / math.sqrt(head_size)

    def attend(n, hooks):
        b = block_of(n)
        shifted_start = length if n <= n_block // 2 else 0
        start = pl.multiple_of(half + sh * (shifted_start - half), half)

        counts = (2 * n - 1, 2 * n)
        strips = (s0_ref, s1_ref)

        def rows_of(r):
            return pl.ds(pl.multiple_of(b * block + r * sub, sub), sub)

        def columns_of(h):
            return pl.ds(pl.multiple_of(h * head_size, head_size), head_size)

        def keys_of(j, wide=1):
            return pl.ds(pl.multiple_of(start + j * sub, sub), wide * sub)

        def score(r, h, j, top):
            wide = min(2, counts[r] - j)
            value = jnp.dot(
                q_ref[rows_of(r), columns_of(h)],
                k_ref[:, keys_of(j, wide)],
                preferred_element_type=jnp.float32,
            )
            for i in range(wide):
                part = value[:, i * sub : (i + 1) * sub]
                if j + i == counts[r] - 1:
                    row_index = lax.broadcasted_iota(jnp.int32, part.shape, 0)
                    key_index = lax.broadcasted_iota(jnp.int32, part.shape, 1)
                    part = jnp.where(key_index <= row_index, part, neg_big)
                strips[r][:, (j + i) * sub : (j + i + 1) * sub] = part
                for c in range(0, sub, 128):
                    lanes = part[:, c : c + 128]
                    top = lanes if top is None else jnp.maximum(top, lanes)
            return top

        def weigh(r, j, wide, top, state):
            weights = jnp.exp2((strips[r][:, j * sub : (j + wide) * sub] - top) * factor)
            term = jnp.dot(
                weights.astype(jnp.bfloat16),
                vt_ref[keys_of(j, wide), :],
                preferred_element_type=jnp.float32,
            )
            return term if state is None else state + term

        def phase(r, h, top, next_r, next_h):
            top = jnp.max(top, axis=1, keepdims=True)
            state, next_top = None, None
            for j in range(0, 2 * n, 2):
                next_top = score(next_r, next_h, j, next_top)
                if j < counts[r]:
                    state = weigh(r, j, min(2, counts[r] - j), top, state)
            context, total = state[:, :head_size], state[:, head_size:]
            attn_ref[rows_of(r), columns_of(h)] = (context * (1.0 / total)).astype(jnp.bfloat16)
            return next_top

        def body(h, top):
            for at, hook in hooks:
                pl.when(h == at)(hook)
            top = phase(0, h, top, 1, h)
            return phase(1, h, top, 0, jnp.minimum(h + 1, n_local - 1))

        first = None
        for j in range(0, counts[0], 2):
            first = score(0, 0, j, first)
        lax.fori_loop(0, n_local, body, first)

    pairs = {}
    attend(2, [(1, back_scatter)])
    pairs[2] = act_part(2)

    @pl.when(sh == 1)
    def _():
        for tail, forward in zip(tails, forwards):
            tail.wait_recv()
            forward.start()

    attend(1, [])
    pairs[1] = act_part(1)

    @pl.when(sh == 1)
    def _():
        for copy in forwards:
            copy.wait_recv()
        for c in range(0, half, block):
            vt_ref[c : c + block, :head_size] = v_ref[:, c : c + block].T

    def early():
        act_scatter(2, pairs[2])
        act_scatter(1, pairs[1])
        back_gather()

    attend(4, [(1, early)])
    pairs[4] = act_part(4)

    def late():
        act_scatter(4, pairs[4])

    def late_gather():
        for n in (2, 4):
            settle(act_in.at[n - 1, pl.ds(0, n_chip - 1)], rs_in_sem.at[n - 1])
        act_gather(1)

    attend(3, [(1, late), (3, late_gather)])
    last_scatter(3)
    back_finish()

    def seq_scatter(value):
        for p in range(n_seq):
            r, c = (p // s_across) * sr, (p % s_across) * sc
            seq_send[p] = value[r : r + sr, c : c + sc]
        seq_in[me_s] = seq_send[me_s]
        for step in range(1, n_seq):
            peer = lax.rem(me_s + step, n_seq)
            remote(
                seq_send.at[peer],
                seq_in.at[me_s],
                seq_send_sem.at[0, 0],
                seq_in_sem.at[0, 0],
                {"seq": peer},
            )

    def seq_gather():
        settle(seq_in.at[pl.ds(0, n_seq - 1)], seq_in_sem.at[0, 0])
        total = seq_in[0]
        for p in range(1, n_seq):
            total = total + seq_in[p]
        seq_all[me_s] = total * adapter_scale
        for step in range(1, n_seq):
            remote(
                seq_all.at[me_s],
                seq_all.at[me_s],
                seq_send_sem.at[0, 1],
                seq_in_sem.at[0, 1],
                {"seq": lax.rem(me_s + step, n_seq)},
            )

    act_finish(1)
    up_total = up_part(1)
    seq_scatter(jnp.dot(back_ref[...], attn_ref[...], preferred_element_type=jnp.float32))
    settle(act_in.at[0, pl.ds(0, n_chip - 1)], rs_in_sem.at[0])
    settle(last_in.at[pl.ds(0, n_head - 1)], rs_in_sem.at[last_step - 1])
    act_gather(0)
    seq_gather()
    act_finish(0)
    low_copy = pltpu.make_async_copy(low_ref, low_hbm, local_sem.at[4])
    low_copy.start()
    up_send[...] = (up_total + up_part(0)).astype(sum_type)
    for step in range(1, n_seq):
        remote(
            up_send,
            up_all.at[me_s],
            seq_send_sem.at[1, 0],
            seq_in_sem.at[1, 0],
            {"seq": lax.rem(me_s + step, n_seq)},
        )
    up_all[me_s] = up_send[...]

    settle(seq_all.at[pl.ds(0, n_seq - 1)], seq_in_sem.at[0, 1])
    for p in range(n_seq):
        r, c = (p // s_across) * sr, (p % s_across) * sc
        down_out[r : r + sr, c : c + sc] = seq_all[p]
    down_copy = pltpu.make_async_copy(down_out, down_hbm, local_sem.at[5])
    down_copy.start()

    settle(up_all.at[pl.ds(0, n_seq - 1)], seq_in_sem.at[1, 0])
    total = up_all[0].astype(jnp.float32)
    for p in range(1, n_seq):
        total = total + up_all[p].astype(jnp.float32)
    up_out[...] = total * adapter_scale

    low_copy.wait()
    down_copy.wait()
    kv_copies[0].wait_send()
    kv_copies[1].wait_send()
    back_pair_copy.wait_send()
    settle(last_send.at[pl.ds(0, n_head - 1)], rs_send_sem.at[last_step - 1])
    for n in pairs:
        pairs[n].wait_send()
        settle(act_send.at[n - 1, pl.ds(0, n_chip - 1)], rs_send_sem.at[n - 1])
    settle(back_send.at[pl.ds(0, n_chip - 1)], rs_send_sem.at[n_block])
    settle(act_all.at[0, pl.ds(0, n_head - 1)], ag_send_sem.at[0])
    settle(act_all.at[1, pl.ds(0, n_head - 1)], ag_send_sem.at[1])
    settle(back_all.at[pl.ds(0, n_head - 1)], ag_send_sem.at[2])
    settle(seq_send.at[pl.ds(0, n_seq - 1)], seq_send_sem.at[0, 0])
    settle(seq_all.at[pl.ds(0, n_seq - 1)], seq_send_sem.at[0, 1])
    settle(up_all.at[pl.ds(0, n_seq - 1)], seq_send_sem.at[1, 0])

    @pl.when(sh == 1)
    def _():
        for copy in tails + forwards:
            copy.wait_send()


def finish(low_ref, down_ref, up_ref, act_out, down_out, up_out):
    act_out[...] = low_ref[...].astype(jnp.float32)
    down_out[...] = down_ref[...]
    up_out[...] = up_ref[...]


def solution(mesh):
    n_seq, n_head = mesh.shape["seq"], mesh.shape["head"]
    n_chip = n_head // 2
    in_specs = (
        P("seq", "head"),
        P("head", "seq"),
        P("head", "seq"),
        P("head", None),
        P(None, "head"),
        P("seq", "head"),
    )
    out_specs = (P(None, "seq"), P("head", None), P(None, "head"))

    def on_device(queries, keys, values, down_factor, up_factor, gradient):
        length, width = queries.shape
        own = keys.shape[0]
        rank = up_factor.shape[0]
        n_block = length // block
        joined = length + length // 2
        pr, pc, _ = pieces_of(rank // 2, block, n_chip)
        sr, sc, _ = pieces_of(rank, block, n_seq)
        f32, b16 = jnp.float32, jnp.bfloat16
        dma = pltpu.SemaphoreType.DMA
        anywhere = pl.BlockSpec(memory_space=pl.ANY)
        vmem = pl.BlockSpec(memory_space=pltpu.VMEM)
        low, down, up = pl.pallas_call(
            functools.partial(kernel, n_seq, n_head),
            out_shape=(
                jax.ShapeDtypeStruct((rank, length), b16),
                jax.ShapeDtypeStruct((rank, width), f32),
                jax.ShapeDtypeStruct((rank, width), f32),
            ),
            in_specs=[anywhere, anywhere, anywhere, vmem, vmem, anywhere],
            out_specs=(anywhere, anywhere, vmem),
            scratch_shapes=[
                pltpu.VMEM((rank, length), b16),
                pltpu.VMEM((rank, width), f32),
                pltpu.VMEM((length, width), b16),
                pltpu.VMEM((length, width), b16),
                pltpu.VMEM((2 * own, joined), b16),
                pltpu.VMEM((2 * own, joined), b16),
                pltpu.VMEM((joined, 4 * own), b16),
                pltpu.VMEM((length, width), b16),
                pltpu.VMEM((2, n_block, rank // 2, block), f32),
                pltpu.VMEM((n_block, rank // 2, block), f32),
                pltpu.VMEM((n_chip, n_block, pr, pc), sum_type),
                pltpu.VMEM((n_chip, n_block, pr, pc), sum_type),
                pltpu.VMEM((n_head, n_block, pr, pc), b16),
                pltpu.VMEM((rank, length), b16),
                pltpu.VMEM((n_block, 2, rank // 2, block), f32),
                pltpu.VMEM((n_block, rank // 2, block), f32),
                pltpu.VMEM((n_block, n_chip, pr, pc), sum_type),
                pltpu.VMEM((n_block, n_chip, pr, pc), sum_type),
                pltpu.VMEM((2, n_head, n_block // 2, pr, pc), b16),
                pltpu.VMEM((n_head, pr, pc), sum_type),
                pltpu.VMEM((n_head, pr, pc), sum_type),
                pltpu.VMEM((block // 2, length), f32),
                pltpu.VMEM((block // 2, length), f32),
                pltpu.VMEM((width, rank), b16),
                pltpu.VMEM((rank, width), sum_type),
                pltpu.VMEM((n_seq, rank, width), sum_type),
                pltpu.VMEM((n_seq, sr, sc), f32),
                pltpu.VMEM((n_seq, sr, sc), f32),
                pltpu.VMEM((n_seq, sr, sc), f32),
                dma((6,)),
                dma((6,)),
                dma((6,)),
                dma((n_block + 1,)),
                dma((n_block + 1,)),
                dma((n_block + 1,)),
                dma((n_block + 1,)),
                dma((3,)),
                dma((3,)),
                dma((2, 2)),
                dma((2, 2)),
            ],
            compiler_params=pltpu.CompilerParams(
                collective_id=0, has_side_effects=True, vmem_limit_bytes=56 * 2**20
            ),
            cost_estimate=pl.CostEstimate(
                flops=6 * 10**9, bytes_accessed=8 * 2**20, transcendentals=10**7
            ),
        )(queries, keys, values, down_factor.T, up_factor, gradient)
        activations, down, up = pl.pallas_call(
            finish,
            out_shape=(
                jax.ShapeDtypeStruct((rank, length), f32),
                jax.ShapeDtypeStruct((rank, width), f32),
                jax.ShapeDtypeStruct((rank, width), f32),
            ),
            in_specs=[vmem, vmem, vmem],
            out_specs=(vmem, vmem, vmem),
        )(low, down, up)
        return activations, down.T, up

    return jax.shard_map(
        on_device, mesh=mesh, in_specs=in_specs, out_specs=out_specs, check_vma=False
    )
```
